32 devices in a mesh: slab: 16 (over z, y, x), coil: 2 (over core).
Axes of the slice: x: 2, y: 2, z: 4, core: 2. Of those that a mesh axis runs over, the one named last changes fastest.
Arguments:
- image: float32 [128, 2, 16, 384], P(('slab', 'coil')), may hold values from -6 to 6
- noise: float32 [128, 2, 16, 384], P(('slab', 'coil')), may hold values from -1.2 to 1.2
- sens: bfloat16 [16, 2, 16, 384, 128], P('coil', None, 'slab'), may hold values from -1 to 1
- measured: bfloat16 [16, 2, 16, 384, 128], P('coil', None, 'slab'), may hold values from -3 to 3
- mask: int32 [384, 128], replicated, may hold values 0 or 1
- w_first: bfloat16 [3, 3, 10, 128], replicated, may hold values from -0.625 to 0.625
- b_first: float32 [128], replicated, may hold values from -3 to 3
- w_second: bfloat16 [128, 128], replicated, may hold values from -0.5 to 0.5
- b_second: float32 [128], replicated, may hold values from -3 to 3
- w_third: bfloat16 [128, 128], replicated, may hold values from -0.5 to 0.5
- b_third: float32 [128], replicated, may hold values from -3 to 3
- w_last: bfloat16 [3, 3, 2, 128], replicated, may hold values from -0.1875 to 0.1875
Outputs:
- updated: float32 [128, 2, 16, 384], P(('slab', 'coil'))
The draws below stay inside these ranges and needn't reach their ends.
Inputs may be any that keep to these rules, and one draw needn't show every extreme that they name: `mask`: 1 where the (ky, kz) line was measured, else 0.
All inputs are finite; a program needn't handle non-finite values.
Results may differ from the reference program's by a relative error of at most 0.0035.
Values may be sent and summed in bfloat16 or wider, within the bound.
No kernel may reach another device: no remote copies, remote signals or barrier semaphores. Data moves between devices by JAX's collectives and lax.ppermute only.
A program may use at most 256 MiB of HBM per device.

```python
import jax
import jax.numpy as jnp
from jax import lax

NY = 384
COILS = 16
WIDTH = 128
XW = 16
NZ = 128


def place_ends(entries, rng, low, high):
    longest = entries.shape.index(max(entries.shape))
    spots = []
    for shift in (0, 1):
        where = [jax.random.randint(jax.random.fold_in(rng, axis), (), 0, length) for axis, length in enumerate(entries.shape)]
        where[longest] = (where[longest] + shift) % entries.shape[longest]
        spots.append(tuple(where))
    return entries.at[spots[0]].set(low).at[spots[1]].set(high)


def steps_of(stream_key, extent, pieces, low, high):
    def one(axis_at, shards_of):
        draws = jax.random.uniform(jax.random.fold_in(jax.random.fold_in(stream_key, 6), axis_at), (shards_of,), jnp.float32, low / len(pieces), high / len(pieces))
        return jnp.repeat(jnp.exp(draws), extent[axis_at] // shards_of).reshape((-1,) + (1,) * (len(extent) - axis_at - 1))

    factor_of = one(*pieces[0])
    for cut in pieces[1:]:
        factor_of = factor_of * one(*cut)
    return factor_of


def scatter_about(own_key, extent, spread, bound, cuts=(), held_as=jnp.bfloat16):
    loudness = steps_of(own_key, extent, cuts, -0.22, 0.18) if cuts else 1.0
    values = jax.random.normal(own_key, extent, jnp.float32) * spread * loudness
    return jnp.minimum(jnp.maximum(values, -bound), bound).astype(held_as)


def setup_inputs(seed: int = 0) -> dict:
    streams_of = jax.random.split(jax.random.key(seed), 13)
    image = scatter_about(streams_of[0], (NZ, 2, XW, NY), 1.0, 6.0, ((0, 32),), jnp.float32)
    noise = scatter_about(streams_of[1], (NZ, 2, XW, NY), 0.2, 1.2, ((0, 32),), jnp.float32)
    sens = scatter_about(streams_of[2], (COILS, 2, XW, NY, NZ), 0.18, 1.0, ((0, 2), (2, 16)))
    measured = scatter_about(streams_of[3], (COILS, 2, XW, NY, NZ), 0.5, 3.0, ((0, 2), (2, 16)))
    mask = place_ends((jax.random.randint(streams_of[4], (NY, NZ), 0, 3) < 1).astype(jnp.int32), jax.random.fold_in(streams_of[4], 1), 0, 1)
    w_first = scatter_about(streams_of[5], (3, 3, 10, WIDTH), 90 ** -0.5, 0.625)
    b_first = scatter_about(streams_of[6], (WIDTH,), 0.5, 3.0, (), jnp.float32)
    w_second = scatter_about(streams_of[7], (WIDTH, WIDTH), WIDTH ** -0.5, 0.5)
    b_second = scatter_about(streams_of[8], (WIDTH,), 0.5, 3.0, (), jnp.float32)
    w_third = scatter_about(streams_of[9], (WIDTH, WIDTH), WIDTH ** -0.5, 0.5)
    b_third = scatter_about(streams_of[10], (WIDTH,), 0.5, 3.0, (), jnp.float32)
    w_last = scatter_about(streams_of[11], (3, 3, 2, WIDTH), (9 * WIDTH) ** -0.5, 0.1875)
    return dict(image=image, noise=noise, sens=sens, measured=measured, mask=mask, w_first=w_first, b_first=b_first, w_second=w_second, b_second=b_second, w_third=w_third, b_third=b_third, w_last=w_last)


STEP_SIZE = 0.5
HIGHEST_MODE = lax.Precision.HIGHEST

def dft_tables(length):
    line_index = jnp.arange(length, dtype=jnp.int32)
    phase_turns = line_index[:, None] * line_index[None, :] % length
    phase_angle = phase_turns.astype(jnp.float32) * (2.0 * jnp.pi / length)
    norm_scale = 1.0 / jnp.sqrt(jnp.float32(length))
    return ((jnp.cos(phase_angle) * norm_scale).astype(jnp.bfloat16), (jnp.sin(phase_angle) * norm_scale).astype(jnp.bfloat16))

def widen(values):
    return lax.optimization_barrier(values).astype(jnp.float32)

def along_y(values, table):
    return jnp.einsum('...yz,yk->...kz', widen(values), widen(table), precision=HIGHEST_MODE)

def along_z(values, table):
    return jnp.einsum('...z,zk->...k', widen(values), widen(table), precision=HIGHEST_MODE)

def spectrum(real_part, imag_part, cos_y, sin_y, cos_z, sin_z, forward):
    sign = 1.0 if forward else -1.0
    out_real = (along_y(real_part, cos_y) + sign * along_y(imag_part, sin_y)).astype(jnp.bfloat16)
    out_imag = (along_y(imag_part, cos_y) - sign * along_y(real_part, sin_y)).astype(jnp.bfloat16)
    last_real = along_z(out_real, cos_z) + sign * along_z(out_imag, sin_z)
    last_imag = along_z(out_imag, cos_z) - sign * along_z(out_real, sin_z)
    return (last_real, last_imag)

def coil_adjoint(planes, coil_sens, coil_data, sampled, tables_all):
    cos_y, sin_y, cos_z, sin_z = tables_all
    sens_real = coil_sens[..., 0, :, :, :].astype(jnp.float32)
    sens_imag = coil_sens[..., 1, :, :, :].astype(jnp.float32)
    image_real = planes[0]
    image_imag = planes[1]
    coil_real = (sens_real * image_real - sens_imag * image_imag).astype(jnp.bfloat16)
    coil_imag = (sens_real * image_imag + sens_imag * image_real).astype(jnp.bfloat16)
    spec_real, spec_imag = spectrum(coil_real, coil_imag, cos_y, sin_y, cos_z, sin_z, True)
    miss_real = (sampled * (spec_real - coil_data[..., 0, :, :, :].astype(jnp.float32))).astype(jnp.bfloat16)
    miss_imag = (sampled * (spec_imag - coil_data[..., 1, :, :, :].astype(jnp.float32))).astype(jnp.bfloat16)
    back_real, back_imag = spectrum(miss_real, miss_imag, cos_y, sin_y, cos_z, sin_z, False)
    return (sens_real * back_real + sens_imag * back_imag, sens_real * back_imag - sens_imag * back_real)

def score_net(window, w_first, b_first, w_second, b_second, w_third, b_third, w_last):
    slice_count = window.shape[0] - 4
    row_count = window.shape[2]
    col_count = window.shape[3]
    stacked = jnp.concatenate([window[offset:offset + slice_count] for offset in range(5)], axis=1)
    framed = jnp.pad(stacked, ((0, 0), (0, 0), (1, 1), (1, 1))).astype(jnp.float32)
    first_sum = jnp.zeros((slice_count, row_count, col_count, w_first.shape[-1]), jnp.float32)
    for shift_x in range(3):
        for shift_y in range(3):
            first_sum = first_sum + jnp.einsum('zcxy,ck->zxyk', framed[:, :, shift_x:shift_x + row_count, shift_y:shift_y + col_count], w_first[shift_x, shift_y].astype(jnp.float32))
    hidden = jax.nn.silu(first_sum + b_first).astype(jnp.bfloat16)
    hidden = jax.nn.silu(jnp.einsum('zxyk,kj->zxyj', hidden.astype(jnp.float32), w_second.astype(jnp.float32)) + b_second).astype(jnp.bfloat16)
    hidden = jax.nn.silu(jnp.einsum('zxyk,kj->zxyj', hidden.astype(jnp.float32), w_third.astype(jnp.float32)) + b_third).astype(jnp.bfloat16)
    framed = jnp.pad(hidden, ((0, 0), (1, 1), (1, 1), (0, 0))).astype(jnp.float32)
    score_field = jnp.zeros((slice_count, 2, row_count, col_count), jnp.float32)
    for shift_x in range(3):
        for shift_y in range(3):
            score_field = score_field + jnp.einsum('zxyk,ok->zoxy', framed[:, shift_x:shift_x + row_count, shift_y:shift_y + col_count], w_last[shift_x, shift_y].astype(jnp.float32))
    return score_field

def reference(image, noise, sens, measured, mask, w_first, b_first, w_second, b_second, w_third, b_third, w_last):
    padded = jnp.pad(image.astype(jnp.bfloat16), ((2, 2), (0, 0), (0, 0), (0, 0)))

    def one_slice(slice_index):
        window = lax.dynamic_slice_in_dim(padded, slice_index, 5, 0)
        return score_net(window, w_first, b_first, w_second, b_second, w_third, b_third, w_last)[0]
    score_field = lax.map(one_slice, jnp.arange(NZ, dtype=jnp.int32))
    planes = jnp.transpose(image, (1, 2, 3, 0))
    cos_y, sin_y = dft_tables(NY)
    cos_z, sin_z = dft_tables(NZ)
    sampled = mask.astype(jnp.float32)

    def add_coil(running_sum, pair):
        part_real, part_imag = coil_adjoint(planes, pair[0], pair[1], sampled, (cos_y, sin_y, cos_z, sin_z))
        return (running_sum + jnp.stack([part_real, part_imag]), None)
    start_sum = jnp.zeros(planes.shape, jnp.float32)
    gradient, _ = lax.scan(add_coil, start_sum, (sens, measured))
    gradient = jnp.transpose(gradient, (3, 0, 1, 2))
    return image + STEP_SIZE * (score_field - gradient) + noise
```

```python
import jax
import jax.numpy as jnp
import numpy as np
from jax import lax
from jax.experimental import pallas as pl
from jax.experimental.pallas import tpu as pltpu
from jax.sharding import PartitionSpec as P

STEP_SIZE = 0.5
F32 = jnp.float32
BF16 = jnp.bfloat16
QUAD = 4
GROUP = 8
VMEM_LIMIT = 24 * 2**20
BUSY = 4 * 10**10


def dot(lhs, rhs):
    return jnp.dot(lhs, rhs, preferred_element_type=F32)


def dot_tn(lhs, rhs):
    return lax.dot_general(lhs, rhs, (((0,), (0,)), ((), ())), preferred_element_type=F32)


def dot_nt(lhs, rhs):
    return lax.dot_general(lhs, rhs, (((1,), (1,)), ((), ())), preferred_element_type=F32)


def dft_table(length):
    index = np.arange(length)
    turns = (index[:, None] * index[None, :]) % length
    angle = turns * (2.0 * np.pi / length)
    scale = 1.0 / np.sqrt(length)
    cos = np.cos(angle) * scale
    sin = np.sin(angle) * scale
    return np.block([[cos, sin], [-sin, cos]]).astype(np.float32).astype(BF16)


def send_order(slices, rows):
    place = np.zeros((rows * slices * 2, slices * 2 * rows), np.float32)
    for z in range(slices):
        for p in range(2):
            for x in range(rows):
                place[(x * slices + z) * 2 + p, (z * 2 + p) * rows + x] = 1
    return place.astype(BF16)


def depth_order(devices, x_local, slices):
    depth = devices * slices
    place = np.zeros((x_local, devices * x_local * slices * 2, 2 * depth), np.float32)
    for d in range(devices):
        for x in range(x_local):
            for z in range(slices):
                for p in range(2):
                    place[x, ((d * x_local + x) * slices + z) * 2 + p, p * depth + d * slices + z] = 1
    return place.reshape(-1, 2 * depth).astype(BF16)


def gather_order(slabs, coils, x_local, slices):
    rows = slabs * x_local
    place = np.zeros((slices * 2 * rows, slabs * coils * x_local * slices * 2), np.float32)
    for s in range(slabs):
        for c in range(coils):
            for x in range(x_local):
                for z in range(slices):
                    for p in range(2):
                        source = (((s * coils + c) * x_local + x) * slices + z) * 2 + p
                        place[(z * 2 + p) * rows + s * x_local + x, source] = 1
    return place.astype(BF16)


def first_order():
    place = np.zeros((3, 5, 2, 8, QUAD, 5, 3, 2, GROUP), np.float32)
    for xo in range(QUAD):
        for a in range(3):
            for b in range(3):
                for o in range(5):
                    for p in range(2):
                        place[a, o, p, b, xo, o, b, p, xo + 1 + a] = 0.5
    return place.reshape(240, QUAD * 240).astype(BF16)


def last_order():
    place = np.zeros((QUAD, 3, 2, GROUP, 3, 3, 8), np.float32)
    for xo in range(QUAD):
        for j in range(GROUP):
            a = xo - j + 3
            if 0 <= a < 3:
                for b in range(3):
                    for o in range(2):
                        place[xo, b, o, j, a, b, o] = 1
    return place.reshape(QUAD * 48, 72).astype(BF16)


HBM = pl.BlockSpec(memory_space=pltpu.HBM)
VMEM = pl.BlockSpec(memory_space=pltpu.VMEM)


def fetch(sources, targets, sems):
    copies = [pltpu.make_async_copy(s, t, sems.at[i]) for i, (s, t) in enumerate(zip(sources, targets))]
    for copy in copies:
        copy.start()
    return copies


def room(*arrays):
    return [pltpu.VMEM(a.shape, a.dtype) for a in arrays] + [pltpu.SemaphoreType.DMA((len(arrays),))]


def call(kernel, out_shape, scratch=(), flops=0, nbytes=0, **kwargs):
    return pl.pallas_call(
        kernel,
        out_shape=out_shape,
        scratch_shapes=list(scratch),
        compiler_params=pltpu.CompilerParams(vmem_limit_bytes=VMEM_LIMIT),
        cost_estimate=pl.CostEstimate(flops=flops, bytes_accessed=nbytes, transcendentals=0),
        **kwargs,
    )


def pack_kernel(image_hbm, order_hbm, blocks_ref, low_ref, high_ref, image_ref, order_ref, sems):
    for copy in fetch((image_hbm, order_hbm), (image_ref, order_ref), sems):
        copy.wait()
    slices, parts, rows, cols = image_ref.shape
    copies = blocks_ref.shape[0] * blocks_ref.shape[1] // (slices * parts * rows)
    image = image_ref[...].astype(BF16)
    moved = dot(order_ref[...], image.reshape(slices * parts * rows, cols))
    slabs = blocks_ref.shape[0] // copies
    moved = moved.reshape(slabs, 1, blocks_ref.shape[1], cols)
    moved = jnp.broadcast_to(moved, (slabs, copies) + moved.shape[2:])
    blocks_ref[...] = moved.reshape(blocks_ref.shape).astype(BF16)
    even = lax.axis_index("coil") % 2 == 0
    first = image_ref[:2]
    last = image_ref[slices - 2 :]
    low_ref[...] = jnp.where(even, last, first).astype(BF16)
    high_ref[...] = jnp.where(even, first, last).astype(BF16)


def fold_weights(sources, targets, rows):
    first_order_ref, last_order_ref, first_ref, b1_ref, second_ref, b2_ref, third_ref, b3_ref, last_ref = sources
    w1_ref, c1_ref, w2_ref, c2_ref, w3_ref, c3_ref, w4_ref = targets
    width = second_ref.shape[0]

    def padded(ref):
        rows[...] = jnp.zeros_like(rows)
        outer, inner, count, _ = ref.shape
        for i in range(outer):
            for j in range(inner):
                rows[i * inner + j, :count] = ref[i, j].astype(F32)
        return rows[: outer * inner].reshape(outer * inner * 8, width).astype(BF16)

    placed = dot_tn(padded(first_ref), first_order_ref[...])
    for xo in range(QUAD):
        w1_ref[xo * width : (xo + 1) * width] = placed[:, xo * 240 : (xo + 1) * 240].astype(BF16)
    placed = dot(last_order_ref[...], padded(last_ref)).astype(BF16)
    for xo in range(QUAD):
        w4_ref[:, xo * width : (xo + 1) * width] = placed[xo * 48 : (xo + 1) * 48]
    for source, target in ((second_ref, w2_ref), (third_ref, w3_ref)):
        turned = (jnp.transpose(source[...].astype(F32)) * 0.5).astype(BF16)
        zeros = jnp.zeros_like(turned)
        target[...] = jnp.concatenate(
            [jnp.concatenate([turned, zeros], axis=1), jnp.concatenate([zeros, turned], axis=1)], axis=0
        )
    for source, target in ((b1_ref, c1_ref), (b2_ref, c2_ref), (b3_ref, c3_ref)):
        target[...] = jnp.transpose(jnp.broadcast_to(source[...] * 0.5, (width, width)))


def staggered(chains):
    waiting, running = list(chains), []
    while waiting or running:
        if waiting:
            running.append(waiting.pop(0))
        for one in running[::-1]:
            if next(one, one) is one:
                running.remove(one)


def half_silu(half):
    return (half + half * jnp.tanh(half)).astype(BF16)


def score_kernel(z_from, z_count, sources, n_ordered, *refs):
    refs, out_ref, scratch = refs[:sources], refs[sources + n_ordered], refs[sources + n_ordered + 1 :]
    folded, rows, scratch = scratch[:7], scratch[7], scratch[8:]
    fold_weights(refs[3:], folded, rows)
    score_slices(z_from, z_count, refs[:3], folded, out_ref, *scratch)


def score_slices(z_from, z_count, planes, weights, out_ref, shifted, windows, sums):
    image_ref, low_ref, high_ref = planes
    w1_ref, c1_ref, w2_ref, c2_ref, w3_ref, c3_ref, w4_ref = weights
    slices, _, rows, cols = image_ref.shape
    quads = rows // QUAD
    width = c1_ref.shape[0]
    even = lax.axis_index("coil") % 2 == 0

    def plane(z, p):
        if 0 <= z < slices:
            return image_ref[z, p].astype(BF16).astype(F32)
        i = z + 2 if z < 0 else z - slices
        one, two = low_ref[i, p].astype(F32), high_ref[i, p].astype(F32)
        return jnp.where(even, two, one) if z < 0 else jnp.where(even, one, two)

    def earlier(values):
        at = lax.broadcasted_iota(jnp.int32, values.shape, 1)
        return jnp.where(at == 0, 0.0, pltpu.roll(values, 1, 1))

    def later(values):
        at = lax.broadcasted_iota(jnp.int32, values.shape, 1)
        return jnp.where(at == cols - 1, 0.0, pltpu.roll(values, cols - 1, 1))

    shifted[...] = jnp.zeros_like(shifted)
    for i in range(z_count + 4):
        for p in range(2):
            values = plane(z_from + i - 2, p)
            for b, moved in enumerate((earlier(values), values, later(values))):
                shifted[b, 4 : 4 + rows] = moved
                for q in range(quads):
                    start = QUAD * q + 2
                    windows[q, i, b, p * GROUP : (p + 1) * GROUP] = shifted[b, start : start + GROUP].astype(BF16)

    spots = [(q, z) for z in range(z_count) for q in range(quads)]
    inputs = jnp.concatenate([windows[q, z : z + 5].reshape(240, cols) for q, z in spots], axis=1)
    pairs = {}

    def bias(ref, lanes):
        return jnp.concatenate([jnp.concatenate([ref[...]] * (lanes // 128), axis=1)] * 2, axis=0)

    def chain(start, stop, pair):
        half = slice(2 * width * pair, 2 * width * (pair + 1))
        lanes = stop - start
        total = dot(w1_ref[half], inputs[:, start:stop])
        yield
        hidden = half_silu(total + bias(c1_ref, lanes))
        yield
        total = dot(w2_ref[...], hidden)
        yield
        hidden = half_silu(total + bias(c2_ref, lanes))
        yield
        total = dot(w3_ref[...], hidden)
        yield
        hidden = half_silu(total + bias(c3_ref, lanes))
        yield
        pairs[start, pair] = dot(w4_ref[:, half], hidden)

    length = len(spots) * cols
    tile = 256
    staggered([chain(n, min(n + tile, length), pair) for n in range(0, length, tile) for pair in range(QUAD // 2)])
    taps = jnp.concatenate(
        [sum(pairs[n, pair] for pair in range(QUAD // 2)) for n in range(0, length, tile)], axis=1
    )
    for i, (q, z) in enumerate(spots):
        part = taps[:, i * cols : (i + 1) * cols]
        total = part[16:32] + earlier(part[:16]) + later(part[32:])
        sums[z, q, 0] = total[:GROUP]
        sums[z, q, 1] = total[GROUP:]
    for z in range(z_count):
        for o in range(2):
            shifted[0] = jnp.zeros_like(shifted[0])
            for q in range(quads):
                start = QUAD * q + 2
                shifted[0, start : start + GROUP] += sums[z, q, o]
            out_ref[z, o] = shifted[0, 4 : 4 + rows]


def adjoint_kernel(
    planes_ref, sens_ref, measured_ref, mask_ref, half_ref, z_ref, out_ref, y_ref
):
    blocks, block_rows, cols = planes_ref.shape
    coils, _, x_local, _, depth = sens_ref.shape
    y_ref[:cols] = half_ref[...]
    y_ref[cols:, :cols] = -half_ref[:, cols:]
    y_ref[cols:, cols:] = half_ref[:, :cols]
    received = planes_ref[...].astype(F32).reshape(blocks * block_rows, cols).astype(BF16)
    z_table = z_ref[: 2 * depth]
    per = max(1, 512 // depth)
    result = None
    for x in range(x_local):
        place = z_ref[2 * depth + x * blocks * block_rows : 2 * depth + (x + 1) * blocks * block_rows]
        planes = dot_tn(received, place)
        image_real = planes[:, :depth]
        image_imag = planes[:, depth:]
        totals = []

        def along_z(half, count):
            for i in range(count):
                at = slice(i * depth, (i + 1) * depth)
                yield dot(jnp.concatenate([half[:cols, at], half[cols:, at]], axis=1), z_table)

        def stack(top, bottom):
            return jnp.concatenate([jnp.concatenate(top, axis=1), jnp.concatenate(bottom, axis=1)], axis=0)

        def chain(group):
            reals, imags = [], []
            for c in group:
                sens_real = sens_ref[c, 0, x].astype(F32)
                sens_imag = sens_ref[c, 1, x].astype(F32)
                reals.append((sens_real * image_real - sens_imag * image_imag).astype(BF16))
                imags.append((sens_real * image_imag + sens_imag * image_real).astype(BF16))
            stacked = stack(reals, imags)
            yield
            half = dot(y_ref[...], stacked).astype(BF16)
            yield
            specs = list(along_z(half, len(group)))
            yield
            reals, imags = [], []
            for spec, c in zip(specs, group):
                sampled = mask_ref[...].astype(F32)
                reals.append((sampled * (spec[:, :depth] - measured_ref[c, 0, x].astype(F32))).astype(BF16))
                imags.append((sampled * (spec[:, depth:] - measured_ref[c, 1, x].astype(F32))).astype(BF16))
            stacked = stack(imags, reals)
            yield
            half = dot(y_ref[...], stacked).astype(BF16)
            yield
            backs = list(along_z(half, len(group)))
            yield
            for back, c in zip(backs, group):
                back_imag = back[:, :depth]
                back_real = back[:, depth:]
                sens_real = sens_ref[c, 0, x].astype(F32)
                sens_imag = sens_ref[c, 1, x].astype(F32)
                real = sens_real * back_real + sens_imag * back_imag
                imag = sens_real * back_imag - sens_imag * back_real
                if totals:
                    real, imag = totals[0] + real, totals[1] + imag
                totals[:] = [real, imag]

        staggered([chain(range(c, min(c + per, coils))) for c in range(0, coils, per)])
        total = jnp.concatenate(totals, axis=1).astype(BF16)
        placed = dot_nt(place, total)
        result = placed if result is None else result + placed
    out_ref[...] = result.reshape(out_ref.shape).astype(BF16)


def final_kernel(image_ref, noise_ref, one_ref, two_ref, back_ref, order_ref, out_ref):
    blocks, block_rows, cols = back_ref.shape
    received = back_ref[...].astype(F32).reshape(blocks * block_rows, cols).astype(BF16)
    gradient = dot(order_ref[...], received).reshape(image_ref.shape)
    cut = one_ref.shape[0]
    out_ref[:cut] = image_ref[:cut] + STEP_SIZE * (one_ref[...] - gradient[:cut]) + noise_ref[:cut]
    out_ref[cut:] = image_ref[cut:] + STEP_SIZE * (two_ref[...] - gradient[cut:]) + noise_ref[cut:]


def on_device(
    image, noise, sens, measured, mask, w_first, b_first, w_second, b_second, w_third, b_third, w_last
):
    slabs = lax.axis_size("slab")
    groups = lax.axis_size("coil")
    devices = slabs * groups
    slices, _, rows, cols = image.shape
    x_local = rows // slabs
    width = w_second.shape[0]
    depth = sens.shape[4]
    both = ("slab", "coil")
    block = jax.ShapeDtypeStruct((devices, x_local * slices * 2, cols), BF16)
    halo = jax.ShapeDtypeStruct((2, 2, rows, cols), BF16)

    order = jnp.asarray(send_order(slices, rows))
    blocks, low, high = call(
        pack_kernel, (block, halo, halo), room(image, order), flops=BUSY, nbytes=10**6, in_specs=[HBM] * 2
    )(image, order)
    pairs = [(i, i ^ 1) for i in range(devices)]
    across = [(i, ((i + 1) ^ 1) - 1) for i in range(1, devices - 1)]
    low = lax.ppermute(low, both, pairs)
    high = lax.ppermute(high, both, across)
    planes = lax.all_to_all(blocks, both, split_axis=0, concat_axis=0, tiled=True)

    cut = slices // 2
    sources = (
        image, low, high, jnp.asarray(first_order()), jnp.asarray(last_order()),
        jnp.transpose(w_first, (0, 2, 1, 3)), b_first[None],
        w_second, b_second[None], w_third, b_third[None], w_last,
    )

    def score(z_from, count, *ordered):
        return call(
            lambda *refs: score_kernel(z_from, count, len(sources), len(ordered), *refs),
            jax.ShapeDtypeStruct((count, 2, rows, cols), F32),
            [
                pltpu.VMEM((QUAD * width, 240), BF16),
                pltpu.VMEM((width, width), F32),
                pltpu.VMEM((2 * width, 2 * width), BF16),
                pltpu.VMEM((width, width), F32),
                pltpu.VMEM((2 * width, 2 * width), BF16),
                pltpu.VMEM((width, width), F32),
                pltpu.VMEM((48, QUAD * width), BF16),
                pltpu.VMEM((30, 8, width), F32),
                pltpu.VMEM((3, rows + 8, cols), F32),
                pltpu.VMEM((rows // QUAD, count + 4, 3, 2 * GROUP, cols), BF16),
                pltpu.VMEM((count, rows // QUAD, 2, GROUP, cols), F32),
            ],
            flops=BUSY,
            nbytes=2 * 10**6,
            in_specs=[VMEM] * len(sources) + [pl.BlockSpec(memory_space=pl.ANY)] * len(ordered),
        )(*sources, *ordered)

    score_one = score(0, cut)
    z_tables = np.concatenate([dft_table(depth).T, depth_order(devices, x_local, slices)], axis=0)
    partial = call(
        adjoint_kernel, block, [pltpu.VMEM((2 * cols, 2 * cols), BF16)], flops=BUSY, nbytes=5 * 10**6, in_specs=[VMEM] * 6
    )(planes, sens, measured, mask, jnp.asarray(dft_table(cols)[:cols]), jnp.asarray(z_tables))
    score_two = score(cut, slices - cut, partial)
    back = lax.all_to_all(partial, both, split_axis=0, concat_axis=0, tiled=True)
    return call(final_kernel, jax.ShapeDtypeStruct(image.shape, F32), nbytes=10**6)(
        image, noise, score_one, score_two, back,
        jnp.asarray(gather_order(slabs, groups, x_local, slices)),
    )


def solution(mesh):
    whole = P(("slab", "coil"), None, None, None)
    by_coil = P("coil", None, "slab", None, None)
    return jax.shard_map(
        on_device,
        mesh=mesh,
        in_specs=(whole, whole, by_coil, by_coil) + (P(),) * 8,
        out_specs=whole,
        check_vma=False,
    )
```

```python
import functools

import jax
import jax.numpy as jnp
import numpy as np
from jax import lax
from jax.experimental import pallas as pl
from jax.experimental.pallas import tpu as pltpu
from jax.sharding import PartitionSpec as P

STEP_SIZE = 0.5
F32 = jnp.float32
BF16 = jnp.bfloat16
QUAD = 4
GROUP = 8
VMEM_LIMIT = 24 * 2**20
WIDE_LIMIT = 100 * 2**19
BUSY = 4 * 10**10
SHORT = BUSY
BAND = 64


def dot(lhs, rhs):
    return jnp.dot(lhs, rhs, preferred_element_type=F32)


def dot_tn(lhs, rhs):
    return lax.dot_general(lhs, rhs, (((0,), (0,)), ((), ())), preferred_element_type=F32)


def dot_nt(lhs, rhs):
    return lax.dot_general(lhs, rhs, (((1,), (1,)), ((), ())), preferred_element_type=F32)


def dft_table(length):
    index = np.arange(length)
    turns = (index[:, None] * index[None, :]) % length
    angle = turns * (2.0 * np.pi / length)
    scale = 1.0 / np.sqrt(length)
    cos = np.cos(angle) * scale
    sin = np.sin(angle) * scale
    return np.block([[cos, sin], [-sin, cos]]).astype(np.float32).astype(BF16)


def depth_order(devices, x_local, slices):
    depth = devices * slices
    place = np.zeros((x_local, devices * x_local * slices * 2, 2 * depth), np.float32)
    for d in range(devices):
        for x in range(x_local):
            for z in range(slices):
                for p in range(2):
                    place[x, ((d * x_local + x) * slices + z) * 2 + p, p * depth + d * slices + z] = 1
    return place.reshape(-1, 2 * depth).astype(BF16)


def gather_order(slabs, coils, x_local, slices):
    rows = slabs * x_local
    place = np.zeros((slices * 2 * rows, slabs * coils * x_local * slices * 2), np.float32)
    for s in range(slabs):
        for c in range(coils):
            for x in range(x_local):
                for z in range(slices):
                    for p in range(2):
                        source = (((s * coils + c) * x_local + x) * slices + z) * 2 + p
                        place[(z * 2 + p) * rows + s * x_local + x, source] = 1
    return place.astype(BF16)


def first_order():
    place = np.zeros((3, 5, 2, 8, 256), np.float32)
    for a in range(3):
        for b in range(3):
            for o in range(5):
                for p in range(2):
                    place[a, o, p, b, ((o * 3 + b) * 2 + p) * GROUP + 1 + a] = 0.5
    return place.reshape(240, 256).astype(BF16)


def last_order():
    place = np.zeros((QUAD, 3, 2, GROUP, 3, 3, 8), np.float32)
    for xo in range(QUAD):
        for j in range(GROUP):
            a = xo - j + 3
            if 0 <= a < 3:
                for b in range(3):
                    for o in range(2):
                        place[xo, b, o, j, a, b, o] = 1
    return place.reshape(QUAD * 48, 72).astype(BF16)


VMEM = pl.BlockSpec(memory_space=pltpu.VMEM)
HBM = pl.BlockSpec(memory_space=pltpu.HBM)


def call(kernel, out_shape, scratch=(), flops=0, nbytes=0, limit=VMEM_LIMIT, **kwargs):
    return pl.pallas_call(
        kernel,
        out_shape=out_shape,
        scratch_shapes=list(scratch),
        compiler_params=pltpu.CompilerParams(vmem_limit_bytes=limit),
        cost_estimate=pl.CostEstimate(flops=flops, bytes_accessed=nbytes, transcendentals=0),
        **kwargs,
    )


def pack_kernel(image_ref, blocks_ref):
    slices, parts, rows, cols = image_ref.shape
    copies = blocks_ref.shape[0] * blocks_ref.shape[1] // (slices * parts * rows)
    image = image_ref[...].astype(BF16)
    count = slices * parts * rows
    after = lax.broadcasted_iota(jnp.int32, (count, count), 0)
    before = lax.broadcasted_iota(jnp.int32, (count, count), 1)
    source = lax.rem(after, slices * parts) * rows + lax.div(after, slices * parts)
    order = jnp.where(source == before, 1.0, 0.0).astype(BF16)
    moved = dot(order, image.reshape(count, cols))
    slabs = blocks_ref.shape[0] // copies
    moved = moved.reshape(slabs, 1, blocks_ref.shape[1], cols)
    moved = jnp.broadcast_to(moved, (slabs, copies) + moved.shape[2:])
    blocks_ref[...] = moved.reshape(blocks_ref.shape).astype(BF16)


def halo_kernel(outward, image_ref, after_ref, out_ref):
    del after_ref
    slices = image_ref.shape[0]
    even = lax.axis_index("coil") % 2 == 0
    out_ref[...] = jnp.where(even != outward, image_ref[slices - 2 :], image_ref[:2]).astype(BF16)


def fold_weights(sources, targets, rows):
    first_order_ref, last_order_ref, first_ref, b1_ref, second_ref, b2_ref, third_ref, b3_ref, last_ref = sources
    w1_ref, c1_ref, w2_ref, c2_ref, w3_ref, c3_ref, w4_ref = targets
    width = second_ref.shape[0]

    def padded(ref):
        rows[...] = jnp.zeros_like(rows)
        outer, inner, count, _ = ref.shape
        for i in range(outer):
            for j in range(inner):
                rows[i * inner + j, :count] = ref[i, j].astype(F32)
        return rows[: outer * inner].reshape(outer * inner * 8, width).astype(BF16)

    placed = dot_tn(padded(first_ref), first_order_ref[...])
    for xo in range(QUAD):
        moved = pltpu.roll(placed, xo, 1) if xo else placed
        w1_ref[xo * width : (xo + 1) * width] = moved[:, :240].astype(BF16)
    placed = dot(last_order_ref[...], padded(last_ref)).astype(BF16)
    for xo in range(QUAD):
        w4_ref[:, xo * width : (xo + 1) * width] = placed[xo * 48 : (xo + 1) * 48]
    for source, target in ((second_ref, w2_ref), (third_ref, w3_ref)):
        turned = (jnp.transpose(source[...].astype(F32)) * 0.5).astype(BF16)
        zeros = jnp.zeros_like(turned)
        target[...] = jnp.concatenate(
            [jnp.concatenate([turned, zeros], axis=1), jnp.concatenate([zeros, turned], axis=1)], axis=0
        )
    for source, target in ((b1_ref, c1_ref), (b2_ref, c2_ref), (b3_ref, c3_ref)):
        target[...] = jnp.transpose(jnp.broadcast_to(source[...] * 0.5, (width, width)))


def staggered(chains):
    waiting, running = list(chains), []
    while waiting or running:
        if waiting:
            running.append(waiting.pop(0))
        for one in running[::-1]:
            if next(one, one) is one:
                running.remove(one)


def half_silu(half):
    return (half + half * jnp.tanh(half)).astype(BF16)


def score_kernel(starts, z_count, sources, n_ordered, *refs):
    refs, out_ref, scratch = refs[:sources], refs[sources + n_ordered], refs[sources + n_ordered + 1 :]
    folded, rows, scratch = scratch[:7], scratch[7], scratch[8:]
    fold_weights(refs[3:], folded, rows)
    score_slices(starts, z_count, refs[:3], folded, out_ref, *scratch)


def score_slices(starts, z_count, planes, weights, out_ref, shifted, windows):
    image_ref, low_ref, high_ref = planes
    w1_ref, c1_ref, w2_ref, c2_ref, w3_ref, c3_ref, w4_ref = weights
    slices, _, rows, cols = image_ref.shape
    quads = rows // QUAD
    width = c1_ref.shape[0]
    even = lax.axis_index("coil") % 2 == 0

    def plane_at(z, p, below_ref, above_ref):
        if 0 <= z < slices:
            return image_ref[z, p].astype(BF16).astype(F32)
        ref, at = (below_ref, z + 2) if z < 0 else (above_ref, z - slices)
        return ref[at, p].astype(F32)

    def plane(i, p):
        return jnp.where(
            even,
            plane_at(starts[0] + i - 2, p, high_ref, low_ref),
            plane_at(starts[1] + i - 2, p, low_ref, high_ref),
        )

    def earlier(values):
        at = lax.broadcasted_iota(jnp.int32, values.shape, 1)
        return jnp.where(at == 0, 0.0, pltpu.roll(values, 1, 1))

    def later(values):
        at = lax.broadcasted_iota(jnp.int32, values.shape, 1)
        return jnp.where(at == cols - 1, 0.0, pltpu.roll(values, cols - 1, 1))

    shifted[...] = jnp.zeros_like(shifted)
    for i in range(z_count + 4):
        for p in range(2):
            values = plane(i, p)
            for b, moved in enumerate((earlier(values), values, later(values))):
                shifted[b, 4 : 4 + rows] = moved
                for q in range(quads):
                    start = QUAD * q + 2
                    windows[q, i, b, p * GROUP : (p + 1) * GROUP] = shifted[b, start : start + GROUP].astype(BF16)

    spots = [(q, z) for z in range(z_count) for q in range(quads)]
    inputs = jnp.concatenate([windows[q, z : z + 5].reshape(240, cols) for q, z in spots], axis=1)
    taps = {}
    fields = {}
    row = lax.broadcasted_iota(jnp.int32, (GROUP, cols), 0)

    def add_spot(i):
        q, z = spots[i]
        first, last = i * cols, (i + 1) * cols
        part = jnp.concatenate(
            [
                taps[n][:, max(first, n) - n : min(last, n + tile) - n]
                for n in range(first - first % tile, last, tile)
            ],
            axis=1,
        )
        total = part[16:32] + earlier(part[:16]) + later(part[32:])
        start = QUAD * q - 2
        for o in range(2):
            moved = pltpu.roll(total[o * GROUP : (o + 1) * GROUP], start % GROUP, 0)
            for t, keep in ((start // GROUP, row >= start % GROUP), (start // GROUP + 1, row < start % GROUP)):
                if 0 <= t < rows // GROUP:
                    field = fields.get((z, o, t))
                    piece = jnp.where(keep, moved, 0.0)
                    fields[z, o, t] = piece if field is None else field + piece
        if q == quads - 1:
            for o in range(2):
                for t in range(rows // GROUP):
                    out_ref[z, o, t * GROUP : (t + 1) * GROUP] = fields.pop((z, o, t))

    def bias(ref, lanes):
        return jnp.concatenate([jnp.concatenate([ref[...]] * (lanes // 128), axis=1)] * 2, axis=0)

    def chain(start, stop, pair):
        half = slice(2 * width * pair, 2 * width * (pair + 1))
        lanes = stop - start
        total = dot(w1_ref[half], inputs[:, start:stop])
        yield
        hidden = half_silu(total + bias(c1_ref, lanes))
        yield
        total = dot(w2_ref[...], hidden)
        yield
        hidden = half_silu(total + bias(c2_ref, lanes))
        yield
        total = dot(w3_ref[...], hidden)
        yield
        hidden = half_silu(total + bias(c3_ref, lanes))
        yield
        part = dot(w4_ref[:, half], hidden)
        if pair == 0:
            taps[start] = part
            return
        taps[start] = taps[start] + part
        while done[0] < len(spots) and stop >= (done[0] + 1) * cols:
            add_spot(done[0])
            done[0] += 1

    done = [0]
    length = len(spots) * cols
    tile = 256
    staggered([chain(n, min(n + tile, length), pair) for n in range(0, length, tile) for pair in range(QUAD // 2)])

def adjoint_kernel(
    planes_ref, sens_ref, measured_hbm, mask_ref, half_ref, z_ref, out_ref, y_ref, measured_ref, sems
):
    blocks, block_rows, cols = planes_ref.shape
    coils, _, x_local, _, depth = sens_ref.shape
    per = max(1, 512 // depth)
    groups = [range(c, min(c + per, coils)) for c in range(0, coils, per)]
    arrivals = {}
    for i, group in enumerate(groups):
        part = pl.ds(group[0], len(group))
        arrivals[group] = pltpu.make_async_copy(measured_hbm.at[part], measured_ref.at[part], sems.at[i])
        arrivals[group].start()
    y_ref[:cols] = half_ref[...]
    y_ref[cols:, :cols] = -half_ref[:, cols:]
    y_ref[cols:, cols:] = half_ref[:, :cols]
    received = planes_ref[...].astype(F32).reshape(blocks * block_rows, cols).astype(BF16)
    z_table = z_ref[: 2 * depth]
    result = None
    for x in range(x_local):
        place = z_ref[2 * depth + x * blocks * block_rows : 2 * depth + (x + 1) * blocks * block_rows]
        planes = dot_tn(received, place)
        image_real = planes[:, :depth]
        image_imag = planes[:, depth:]
        totals = {}

        def along_z(half, count):
            for i in range(count):
                at = slice(i * depth, (i + 1) * depth)
                yield dot(jnp.concatenate([half[:cols, at], half[cols:, at]], axis=1), z_table)

        def stack(top, bottom):
            return jnp.concatenate([jnp.concatenate(top, axis=1), jnp.concatenate(bottom, axis=1)], axis=0)

        bands = [slice(r, min(r + BAND, cols)) for r in range(0, cols, BAND)]

        def chain(group):
            reals = {c: [] for c in group}
            imags = {c: [] for c in group}

            def joined(parts):
                return [jnp.concatenate(parts[c], axis=0) for c in group]

            for band in bands:
                for c in group:
                    sens_real = sens_ref[c, 0, x, band].astype(F32)
                    sens_imag = sens_ref[c, 1, x, band].astype(F32)
                    reals[c].append((sens_real * image_real[band] - sens_imag * image_imag[band]).astype(BF16))
                    imags[c].append((sens_real * image_imag[band] + sens_imag * image_real[band]).astype(BF16))
            stacked = stack(joined(reals), joined(imags))
            yield
            half = dot(y_ref[...], stacked).astype(BF16)
            yield
            specs = list(along_z(half, len(group)))
            yield
            if x == 0:
                arrivals[group].wait()
            reals = {c: [] for c in group}
            imags = {c: [] for c in group}
            for band in bands:
                sampled = mask_ref[band].astype(F32)
                for spec, c in zip(specs, group):
                    measured_real = measured_ref[c, 0, x, band].astype(F32)
                    measured_imag = measured_ref[c, 1, x, band].astype(F32)
                    reals[c].append((sampled * (spec[band, :depth] - measured_real)).astype(BF16))
                    imags[c].append((sampled * (spec[band, depth:] - measured_imag)).astype(BF16))
            stacked = stack(joined(imags), joined(reals))
            yield
            half = dot(y_ref[...], stacked).astype(BF16)
            yield
            backs = list(along_z(half, len(group)))
            yield
            for band in bands:
                real = imag = None
                for back, c in zip(backs, group):
                    back_imag = back[band, :depth]
                    back_real = back[band, depth:]
                    sens_real = sens_ref[c, 0, x, band].astype(F32)
                    sens_imag = sens_ref[c, 1, x, band].astype(F32)
                    one = sens_real * back_real + sens_imag * back_imag
                    two = sens_real * back_imag - sens_imag * back_real
                    real, imag = (one, two) if real is None else (real + one, imag + two)
                totals.setdefault(band.start, []).append((real, imag))

        staggered([chain(group) for group in groups])
        total = jnp.concatenate(
            [
                jnp.concatenate([sum(t[part] for t in totals[band.start]) for part in range(2)], axis=1)
                for band in bands
            ],
            axis=0,
        ).astype(BF16)
        placed = dot_nt(place, total)
        result = placed if result is None else result + placed
    out_ref[...] = result.reshape(out_ref.shape).astype(BF16)


def final_kernel(image_ref, noise_ref, one_ref, two_ref, back_ref, order_ref, out_ref):
    blocks, block_rows, cols = back_ref.shape
    received = back_ref[...].astype(F32).reshape(blocks * block_rows, cols).astype(BF16)
    gradient = dot(order_ref[...], received).reshape(image_ref.shape)
    slices = image_ref.shape[0]
    cut = one_ref.shape[0]
    even = lax.axis_index("coil") % 2 == 0
    for z in range(slices):
        at_even = two_ref[z] if z < slices - cut else one_ref[z - (slices - cut)]
        at_odd = one_ref[z] if z < cut else two_ref[z - cut]
        field = jnp.where(even, at_even, at_odd)
        out_ref[z] = image_ref[z] + STEP_SIZE * (field - gradient[z]) + noise_ref[z]


def on_device(
    image, noise, sens, measured, mask, w_first, b_first, w_second, b_second, w_third, b_third, w_last
):
    slabs = lax.axis_size("slab")
    groups = lax.axis_size("coil")
    devices = slabs * groups
    slices, _, rows, cols = image.shape
    x_local = rows // slabs
    width = w_second.shape[0]
    depth = sens.shape[4]
    both = ("slab", "coil")
    block = jax.ShapeDtypeStruct((devices, x_local * slices * 2, cols), BF16)

    blocks = call(pack_kernel, block, flops=BUSY, nbytes=10**6, in_specs=[VMEM])(image)
    pairs = [(i, i ^ 1) for i in range(devices)]
    across = [(i, ((i + 1) ^ 1) - 1) for i in range(1, devices - 1)]

    def halo(outward, after):
        kernel = functools.partial(halo_kernel, outward)
        shape = jax.ShapeDtypeStruct((2, 2, rows, cols), BF16)
        slab = call(
            kernel, shape, flops=BUSY, nbytes=10**6, in_specs=[VMEM, pl.BlockSpec(memory_space=pl.ANY)]
        )(image, after)
        return lax.ppermute(slab, both, across if outward else pairs)

    low = halo(False, blocks)
    planes = lax.all_to_all(blocks, both, split_axis=0, concat_axis=0, tiled=True)

    cut = max(1, slices // 4)
    weights = (
        jnp.asarray(first_order()), jnp.asarray(last_order()),
        jnp.transpose(w_first, (0, 2, 1, 3)), b_first[None],
        w_second, b_second[None], w_third, b_third[None], w_last,
    )

    def score(starts, count, flops, planes, *ordered):
        sources = planes + weights
        return call(
            lambda *refs: score_kernel(starts, count, len(sources), len(ordered), *refs),
            jax.ShapeDtypeStruct((count, 2, rows, cols), F32),
            [
                pltpu.VMEM((QUAD * width, 240), BF16),
                pltpu.VMEM((width, width), F32),
                pltpu.VMEM((2 * width, 2 * width), BF16),
                pltpu.VMEM((width, width), F32),
                pltpu.VMEM((2 * width, 2 * width), BF16),
                pltpu.VMEM((width, width), F32),
                pltpu.VMEM((48, QUAD * width), BF16),
                pltpu.VMEM((30, 8, width), F32),
                pltpu.VMEM((3, rows + 8, cols), F32),
                pltpu.VMEM((rows // QUAD, count + 4, 3, 2 * GROUP, cols), BF16),
            ],
            flops=flops,
            nbytes=2 * 10**6,
            in_specs=[VMEM] * len(sources) + [pl.BlockSpec(memory_space=pl.ANY)] * len(ordered),
        )(*sources, *ordered)

    apart = slices - cut >= 2
    high = None if apart else halo(True, blocks)
    score_one = score((slices - cut, 0), cut, SHORT, (image, low, low if apart else high))
    if apart:
        high = halo(True, score_one)
    z_tables = np.concatenate([dft_table(depth).T, depth_order(devices, x_local, slices)], axis=0)
    partial = call(
        adjoint_kernel, block, [pltpu.VMEM((2 * cols, 2 * cols), BF16), pltpu.VMEM(measured.shape, BF16),
         pltpu.SemaphoreType.DMA((sens.shape[0],))],
        flops=BUSY, nbytes=5 * 10**6, limit=WIDE_LIMIT, in_specs=[VMEM] * 2 + [HBM] + [VMEM] * 3
    )(planes, sens, measured, mask, jnp.asarray(dft_table(cols)[:cols]), jnp.asarray(z_tables))
    score_two = score((0, cut), slices - cut, BUSY, (image, low, high), partial)
    back = lax.all_to_all(partial, both, split_axis=0, concat_axis=0, tiled=True)
    return call(final_kernel, jax.ShapeDtypeStruct(image.shape, F32), nbytes=10**6)(
        image, noise, score_one, score_two, back,
        jnp.asarray(gather_order(slabs, groups, x_local, slices)),
    )


def solution(mesh):
    whole = P(("slab", "coil"), None, None, None)
    by_coil = P("coil", None, "slab", None, None)
    return jax.shard_map(
        on_device,
        mesh=mesh,
        in_specs=(whole, whole, by_coil, by_coil) + (P(),) * 8,
        out_specs=whole,
        check_vma=False,
    )
```

```python
import functools

import jax
import jax.numpy as jnp
import numpy as np
from jax import lax
from jax.experimental import pallas as pl
from jax.experimental.pallas import tpu as pltpu
from jax.sharding import PartitionSpec as P

STEP_SIZE = 0.5
F32 = jnp.float32
BF16 = jnp.bfloat16
QUAD = 4
GROUP = 8
VMEM_LIMIT = 24 * 2**20
WIDE_LIMIT = 100 * 2**19
BUSY = 4 * 10**10
SHORT = BUSY
BAND = 64
EARLY = 2


def dot(lhs, rhs):
    return jnp.dot(lhs, rhs, preferred_element_type=F32)


def dot_tn(lhs, rhs):
    return lax.dot_general(lhs, rhs, (((0,), (0,)), ((), ())), preferred_element_type=F32)


def dot_nt(lhs, rhs):
    return lax.dot_general(lhs, rhs, (((1,), (1,)), ((), ())), preferred_element_type=F32)


def dft_table(length):
    index = np.arange(length)
    turns = (index[:, None] * index[None, :]) % length
    angle = turns * (2.0 * np.pi / length)
    scale = 1.0 / np.sqrt(length)
    cos = np.cos(angle) * scale
    sin = np.sin(angle) * scale
    return np.block([[cos, sin], [-sin, cos]]).astype(np.float32).astype(BF16)


def depth_order(devices, x_local, slices):
    depth = devices * slices
    place = np.zeros((x_local, devices * x_local * slices * 2, 2 * depth), np.float32)
    for d in range(devices):
        for x in range(x_local):
            for z in range(slices):
                for p in range(2):
                    place[x, ((d * x_local + x) * slices + z) * 2 + p, p * depth + d * slices + z] = 1
    return place.reshape(-1, 2 * depth).astype(BF16)


def gather_order(slabs, coils, x_local, slices):
    rows = slabs * x_local
    place = np.zeros((slices * 2 * rows, slabs * coils * x_local * slices * 2), np.float32)
    for s in range(slabs):
        for c in range(coils):
            for x in range(x_local):
                for z in range(slices):
                    for p in range(2):
                        source = (((s * coils + c) * x_local + x) * slices + z) * 2 + p
                        place[(z * 2 + p) * rows + s * x_local + x, source] = 1
    return place.astype(BF16)


VMEM = pl.BlockSpec(memory_space=pltpu.VMEM)
HBM = pl.BlockSpec(memory_space=pltpu.HBM)


def call(kernel, out_shape, scratch=(), flops=0, nbytes=0, limit=VMEM_LIMIT, **kwargs):
    return pl.pallas_call(
        kernel,
        out_shape=out_shape,
        scratch_shapes=list(scratch),
        compiler_params=pltpu.CompilerParams(vmem_limit_bytes=limit),
        cost_estimate=pl.CostEstimate(flops=flops, bytes_accessed=nbytes, transcendentals=0),
        **kwargs,
    )


def split(values, count):
    if count & (count - 1) == 0:
        return values & (count - 1), lax.shift_right_logical(values, count.bit_length() - 1)
    return lax.rem(values, count), lax.div(values, count)


def pack_kernel(image_ref, blocks_ref):
    slices, parts, rows, cols = image_ref.shape
    copies = blocks_ref.shape[0] * blocks_ref.shape[1] // (slices * parts * rows)
    image = image_ref[...].astype(BF16)
    count = slices * parts * rows
    after = lax.broadcasted_iota(jnp.int32, (count, count), 0)
    before = lax.broadcasted_iota(jnp.int32, (count, count), 1)
    part, x = split(after, slices * parts)
    source_x, source_part = split(before, rows)
    order = jnp.where((part == source_part) & (x == source_x), 1.0, 0.0).astype(BF16)
    moved = dot(order, image.reshape(count, cols))
    slabs = blocks_ref.shape[0] // copies
    moved = moved.reshape(slabs, 1, blocks_ref.shape[1], cols)
    moved = jnp.broadcast_to(moved, (slabs, copies) + moved.shape[2:])
    blocks_ref[...] = moved.reshape(blocks_ref.shape).astype(BF16)


def halo_kernel(outward, image_ref, after_ref, out_ref):
    del after_ref
    slices = image_ref.shape[0]
    even = lax.axis_index("coil") % 2 == 0
    out_ref[...] = jnp.where(even != outward, image_ref[slices - 2 :], image_ref[:2]).astype(BF16)


def by_three(values):
    return lax.shift_right_logical(values * 11, 5)


def first_order():
    row = lax.broadcasted_iota(jnp.int32, (240, 256), 0)
    col = lax.broadcasted_iota(jnp.int32, (240, 256), 1)
    tap = lax.shift_right_logical(row, 3)
    a = jnp.where(tap >= 20, 2, jnp.where(tap >= 10, 1, 0))
    channel = tap - 10 * a
    group = lax.shift_right_logical(col, 3)
    offset = by_three(lax.shift_right_logical(group, 1))
    b = lax.shift_right_logical(group, 1) - 3 * offset
    same = (channel == 2 * offset + (group & 1)) & ((row & 7) == b) & ((col & 7) == a + 1)
    return jnp.where(same, 0.5, 0.0).astype(BF16)


def last_order():
    row = lax.broadcasted_iota(jnp.int32, (QUAD * 48, 72), 0)
    col = lax.broadcasted_iota(jnp.int32, (QUAD * 48, 72), 1)
    group = lax.shift_right_logical(row, 3)
    xo = by_three(lax.shift_right_logical(group, 1))
    b = lax.shift_right_logical(group, 1) - 3 * xo
    tap = lax.shift_right_logical(col, 3)
    a = by_three(tap)
    same = ((col & 7) == (group & 1)) & (tap - 3 * a == b) & (a == xo - (row & 7) + 3)
    return jnp.where(same, 1.0, 0.0).astype(BF16)


def fold_weights(sources, targets, rows):
    first_ref, b1_ref, second_ref, b2_ref, third_ref, b3_ref, last_ref = sources
    w1_ref, _, w2_ref, c2_ref, w3_ref, c3_ref, w4_ref = targets
    width = second_ref.shape[0]

    def padded(ref):
        rows[...] = jnp.zeros_like(rows)
        outer, inner, count, _ = ref.shape
        for i in range(outer):
            for j in range(inner):
                rows[i * inner + j, :count] = ref[i, j].astype(F32)
        return rows[: outer * inner].reshape(outer * inner * 8, width).astype(BF16)

    rest = jnp.transpose(jnp.broadcast_to(b1_ref[...] * 0.5, (width, width)))
    rest = jnp.concatenate([rest, rest], axis=1)
    lane = lax.broadcasted_iota(jnp.int32, rest.shape, 1)
    column = jnp.zeros_like(rest)
    for k in range(3):
        part = rest.astype(BF16).astype(F32)
        rest = rest - part
        column = jnp.where(lane == 240 + k, part, column)
    placed = dot_tn(padded(first_ref), first_order())
    for xo in range(QUAD):
        moved = pltpu.roll(placed, xo, 1) if xo else placed
        w1_ref[xo * width : (xo + 1) * width] = (moved + column).astype(BF16)
    placed = dot(last_order(), padded(last_ref)).astype(BF16)
    for xo in range(QUAD):
        w4_ref[:, xo * width : (xo + 1) * width] = placed[xo * 48 : (xo + 1) * 48]
    for source, target in ((second_ref, w2_ref), (third_ref, w3_ref)):
        turned = (jnp.transpose(source[...].astype(F32)) * 0.5).astype(BF16)
        zeros = jnp.zeros_like(turned)
        target[...] = jnp.concatenate(
            [jnp.concatenate([turned, zeros], axis=1), jnp.concatenate([zeros, turned], axis=1)], axis=0
        )
    for source, target in ((b2_ref, c2_ref), (b3_ref, c3_ref)):
        target[...] = jnp.transpose(jnp.broadcast_to(source[...] * 0.5, (width, width)))


def staggered(chains):
    waiting, running = list(chains), []
    while waiting or running:
        if waiting:
            running.append(waiting.pop(0))
        for one in running[::-1]:
            if next(one, one) is one:
                running.remove(one)


def half_silu(half):
    return (half + half * jnp.tanh(half)).astype(BF16)


def score_kernel(spots, sources, n_ordered, *refs):
    refs, out_ref, scratch = refs[:sources], refs[sources + n_ordered], refs[sources + n_ordered + 1 :]
    folded, rows, scratch = scratch[:7], scratch[7], scratch[8:]
    fold_weights(refs[3:], folded, rows)
    score_spots(spots, refs[:3], folded, out_ref, *scratch)


def score_spots(spots, planes, weights, out_ref, shifted, windows):
    image_ref, low_ref, high_ref = planes
    w1_ref, w2_ref, c2_ref, w3_ref, c3_ref, w4_ref = weights[:1] + weights[2:]
    slices, _, rows, cols = image_ref.shape
    quads = rows // QUAD
    width = c2_ref.shape[0]
    count = out_ref.shape[0]
    even = lax.axis_index("coil") % 2 == 0

    def plane_at(z, p, below_ref, above_ref):
        if 0 <= z < slices:
            return image_ref[z, p].astype(BF16).astype(F32)
        ref, at = (below_ref, z + 2) if z < 0 else (above_ref, z - slices)
        return ref[at, p].astype(F32)

    def plane(i, p):
        return jnp.where(
            even,
            plane_at(slices - count + i - 2, p, high_ref, low_ref),
            plane_at(i - 2, p, low_ref, high_ref),
        )

    def earlier(values):
        at = lax.broadcasted_iota(jnp.int32, values.shape, 1)
        return jnp.where(at == 0, 0.0, pltpu.roll(values, 1, 1))

    def later(values):
        at = lax.broadcasted_iota(jnp.int32, values.shape, 1)
        return jnp.where(at == cols - 1, 0.0, pltpu.roll(values, cols - 1, 1))

    shifted[...] = jnp.zeros_like(shifted)
    for i in range(count + 4):
        for p in range(2):
            values = plane(i, p)
            for b, moved in enumerate((earlier(values), values, later(values))):
                shifted[b, 4 : 4 + rows] = moved
                for q in range(quads):
                    start = QUAD * q + 2
                    windows[q, i, b, p * GROUP : (p + 1) * GROUP] = shifted[b, start : start + GROUP].astype(BF16)

    place = [jnp.where(even, count - 1 - i, i) for i in range(count)]
    ones = jnp.ones((16, cols), BF16)
    inputs = jnp.concatenate(
        [
            jnp.concatenate([windows[q, pl.ds(place[i], 5)].reshape(240, cols), ones], axis=0)
            for i, q in spots
        ],
        axis=1,
    )
    taps = {}
    fields = {}
    row = lax.broadcasted_iota(jnp.int32, (GROUP, cols), 0)

    def add_spot(n):
        i, q = spots[n]
        first, last = n * cols, (n + 1) * cols
        part = jnp.concatenate(
            [
                taps[m][:, max(first, m) - m : min(last, m + tile) - m]
                for m in range(first - first % tile, last, tile)
            ],
            axis=1,
        )
        total = part[16:32] + earlier(part[:16]) + later(part[32:])
        start = QUAD * q - 2
        for o in range(2):
            moved = pltpu.roll(total[o * GROUP : (o + 1) * GROUP], start % GROUP, 0)
            for t, keep in ((start // GROUP, row >= start % GROUP), (start // GROUP + 1, row < start % GROUP)):
                if 0 <= t < rows // GROUP:
                    field = fields.get((i, o, t))
                    piece = jnp.where(keep, moved, 0.0)
                    fields[i, o, t] = piece if field is None else field + piece
        if n + 1 == len(spots) or spots[n + 1][0] != i:
            for o in range(2):
                for t in range(rows // GROUP):
                    value = fields.pop((i, o, t), None)
                    value = jnp.zeros((GROUP, cols), F32) if value is None else value
                    out_ref[place[i], o, t * GROUP : (t + 1) * GROUP] = value

    def bias(ref, lanes):
        return jnp.concatenate([jnp.concatenate([ref[...]] * (lanes // 128), axis=1)] * 2, axis=0)

    def chain(start, stop, pair):
        half = slice(2 * width * pair, 2 * width * (pair + 1))
        lanes = stop - start
        total = dot(w1_ref[half], inputs[:, start:stop])
        yield
        hidden = half_silu(total)
        yield
        total = dot(w2_ref[...], hidden)
        yield
        hidden = half_silu(total + bias(c2_ref, lanes))
        yield
        total = dot(w3_ref[...], hidden)
        yield
        hidden = half_silu(total + bias(c3_ref, lanes))
        yield
        part = dot(w4_ref[:, half], hidden)
        if pair == 0:
            taps[start] = part
            return
        taps[start] = taps[start] + part
        while done[0] < len(spots) and stop >= (done[0] + 1) * cols:
            add_spot(done[0])
            done[0] += 1

    done = [0]
    length = len(spots) * cols
    tile = 256
    staggered([chain(n, min(n + tile, length), pair) for n in range(0, length, tile) for pair in range(QUAD // 2)])


def adjoint_kernel(
    planes_ref, sens_ref, measured_hbm, mask_ref, half_ref, z_ref, out_ref, y_ref, measured_ref, sems
):
    blocks, block_rows, cols = planes_ref.shape
    coils, _, x_local, _, depth = sens_ref.shape
    per = max(1, 512 // depth)
    groups = [range(c, min(c + per, coils)) for c in range(0, coils, per)]
    arrivals = {}
    for i, group in enumerate(groups):
        part = pl.ds(group[0], len(group))
        arrivals[group] = pltpu.make_async_copy(measured_hbm.at[part], measured_ref.at[part], sems.at[i])
        arrivals[group].start()
    y_ref[:cols] = half_ref[...]
    y_ref[cols:, :cols] = -half_ref[:, cols:]
    y_ref[cols:, cols:] = half_ref[:, :cols]
    received = planes_ref[...].astype(F32).reshape(blocks * block_rows, cols).astype(BF16)
    z_table = z_ref[: 2 * depth]
    result = None
    for x in range(x_local):
        place = z_ref[2 * depth + x * blocks * block_rows : 2 * depth + (x + 1) * blocks * block_rows]
        planes = dot_tn(received, place)
        image_real = planes[:, :depth]
        image_imag = planes[:, depth:]
        totals = {}

        def along_z(half, count):
            for i in range(count):
                at = slice(i * depth, (i + 1) * depth)
                yield dot(jnp.concatenate([half[:cols, at], half[cols:, at]], axis=1), z_table)

        def stack(top, bottom):
            return jnp.concatenate([jnp.concatenate(top, axis=1), jnp.concatenate(bottom, axis=1)], axis=0)

        bands = [slice(r, min(r + BAND, cols)) for r in range(0, cols, BAND)]

        def chain(group):
            reals = {c: [] for c in group}
            imags = {c: [] for c in group}

            def joined(parts):
                return [jnp.concatenate(parts[c], axis=0) for c in group]

            for band in bands:
                for c in group:
                    sens_real = sens_ref[c, 0, x, band].astype(F32)
                    sens_imag = sens_ref[c, 1, x, band].astype(F32)
                    reals[c].append((sens_real * image_real[band] - sens_imag * image_imag[band]).astype(BF16))
                    imags[c].append((sens_real * image_imag[band] + sens_imag * image_real[band]).astype(BF16))
            stacked = stack(joined(reals), joined(imags))
            yield
            half = dot(y_ref[...], stacked).astype(BF16)
            yield
            specs = list(along_z(half, len(group)))
            yield
            if x == 0:
                arrivals[group].wait()
            reals = {c: [] for c in group}
            imags = {c: [] for c in group}
            for band in bands:
                sampled = mask_ref[band].astype(F32)
                for spec, c in zip(specs, group):
                    measured_real = measured_ref[c, 0, x, band].astype(F32)
                    measured_imag = measured_ref[c, 1, x, band].astype(F32)
                    reals[c].append((sampled * (spec[band, :depth] - measured_real)).astype(BF16))
                    imags[c].append((sampled * (spec[band, depth:] - measured_imag)).astype(BF16))
            stacked = stack(joined(imags), joined(reals))
            yield
            half = dot(y_ref[...], stacked).astype(BF16)
            yield
            backs = list(along_z(half, len(group)))
            yield
            for band in bands:
                real = imag = None
                for back, c in zip(backs, group):
                    back_imag = back[band, :depth]
                    back_real = back[band, depth:]
                    sens_real = sens_ref[c, 0, x, band].astype(F32)
                    sens_imag = sens_ref[c, 1, x, band].astype(F32)
                    one = sens_real * back_real + sens_imag * back_imag
                    two = sens_real * back_imag - sens_imag * back_real
                    real, imag = (one, two) if real is None else (real + one, imag + two)
                totals.setdefault(band.start, []).append((real, imag))

        staggered([chain(group) for group in groups])
        total = jnp.concatenate(
            [
                jnp.concatenate([sum(t[part] for t in totals[band.start]) for part in range(2)], axis=1)
                for band in bands
            ],
            axis=0,
        ).astype(BF16)
        placed = dot_nt(place, total)
        result = placed if result is None else result + placed
    out_ref[...] = result.reshape(out_ref.shape).astype(BF16)


def final_kernel(image_ref, noise_ref, one_ref, two_ref, back_ref, order_ref, out_ref):
    blocks, block_rows, cols = back_ref.shape
    received = back_ref[...].astype(F32).reshape(blocks * block_rows, cols).astype(BF16)
    gradient = dot(order_ref[...], received).reshape(image_ref.shape)
    slices = image_ref.shape[0]
    even = lax.axis_index("coil") % 2 == 0
    for z in range(slices):
        field = two_ref[z]
        if z == 0:
            field = field + jnp.where(even, 0.0, one_ref[0])
        if z == slices - 1:
            field = field + jnp.where(even, one_ref[0], 0.0)
        out_ref[z] = image_ref[z] + STEP_SIZE * (field - gradient[z]) + noise_ref[z]


def on_device(
    image, noise, sens, measured, mask, w_first, b_first, w_second, b_second, w_third, b_third, w_last
):
    slabs = lax.axis_size("slab")
    groups = lax.axis_size("coil")
    devices = slabs * groups
    slices, _, rows, cols = image.shape
    x_local = rows // slabs
    width = w_second.shape[0]
    depth = sens.shape[4]
    both = ("slab", "coil")
    block = jax.ShapeDtypeStruct((devices, x_local * slices * 2, cols), BF16)

    blocks = call(pack_kernel, block, flops=BUSY, nbytes=10**6, in_specs=[VMEM])(image)
    pairs = [(i, i ^ 1) for i in range(devices)]
    across = [(i, ((i + 1) ^ 1) - 1) for i in range(1, devices - 1)]

    def halo(outward, after):
        kernel = functools.partial(halo_kernel, outward)
        shape = jax.ShapeDtypeStruct((2, 2, rows, cols), BF16)
        slab = call(
            kernel, shape, flops=BUSY, nbytes=10**6, in_specs=[VMEM, pl.BlockSpec(memory_space=pl.ANY)]
        )(image, after)
        return lax.ppermute(slab, both, across if outward else pairs)

    low = halo(False, blocks)
    planes = lax.all_to_all(blocks, both, split_axis=0, concat_axis=0, tiled=True)

    weights = (
        jnp.transpose(w_first, (0, 2, 1, 3)), b_first[None],
        w_second, b_second[None], w_third, b_third[None], w_last,
    )

    def score(spots, count, flops, planes, *ordered):
        sources = planes + weights
        return call(
            lambda *refs: score_kernel(spots, len(sources), len(ordered), *refs),
            jax.ShapeDtypeStruct((count, 2, rows, cols), F32),
            [
                pltpu.VMEM((QUAD * width, 256), BF16),
                pltpu.VMEM((8, width), F32),
                pltpu.VMEM((2 * width, 2 * width), BF16),
                pltpu.VMEM((width, width), F32),
                pltpu.VMEM((2 * width, 2 * width), BF16),
                pltpu.VMEM((width, width), F32),
                pltpu.VMEM((48, QUAD * width), BF16),
                pltpu.VMEM((30, 8, width), F32),
                pltpu.VMEM((3, rows + 8, cols), F32),
                pltpu.VMEM((rows // QUAD, count + 4, 3, 2 * GROUP, cols), BF16),
            ],
            flops=flops,
            nbytes=2 * 10**6,
            in_specs=[VMEM] * len(sources) + [pl.BlockSpec(memory_space=pl.ANY)] * len(ordered),
        )(*sources, *ordered)

    spots = [(i, q) for i in range(slices) for q in range(rows // QUAD)]
    early = rows // QUAD * EARLY // 4
    apart = slices >= 3
    high = None if apart else halo(True, blocks)
    score_one = score(spots[:early], 1, SHORT, (image, low, low if apart else high))
    if apart:
        high = halo(True, score_one)
    z_tables = np.concatenate([dft_table(depth).T, depth_order(devices, x_local, slices)], axis=0)
    partial = call(
        adjoint_kernel, block, [pltpu.VMEM((2 * cols, 2 * cols), BF16), pltpu.VMEM(measured.shape, BF16),
         pltpu.SemaphoreType.DMA((sens.shape[0],))],
        flops=BUSY, nbytes=5 * 10**6, limit=WIDE_LIMIT, in_specs=[VMEM] * 2 + [HBM] + [VMEM] * 3
    )(planes, sens, measured, mask, jnp.asarray(dft_table(cols)[:cols]), jnp.asarray(z_tables))
    score_two = score(spots[early:], slices, BUSY, (image, low, high), partial)
    back = lax.all_to_all(partial, both, split_axis=0, concat_axis=0, tiled=True)
    return call(final_kernel, jax.ShapeDtypeStruct(image.shape, F32), nbytes=10**6)(
        image, noise, score_one, score_two, back,
        jnp.asarray(gather_order(slabs, groups, x_local, slices)),
    )


def solution(mesh):
    whole = P(("slab", "coil"), None, None, None)
    by_coil = P("coil", None, "slab", None, None)
    return jax.shard_map(
        on_device,
        mesh=mesh,
        in_specs=(whole, whole, by_coil, by_coil) + (P(),) * 8,
        out_specs=whole,
        check_vma=False,
    )
```

```python
import functools

import jax
import jax.numpy as jnp
import numpy as np
from jax import lax
from jax.experimental import pallas as pl
from jax.experimental.pallas import tpu as pltpu
from jax.sharding import PartitionSpec as P

STEP_SIZE = 0.5
F32 = jnp.float32
BF16 = jnp.bfloat16
QUAD = 4
GROUP = 8
VMEM_LIMIT = 24 * 2**20
WIDE_LIMIT = 100 * 2**19
BUSY = 4 * 10**10
SHORT = BUSY
BAND = 64
EARLY = 2


def dot(lhs, rhs):
    return jnp.dot(lhs, rhs, preferred_element_type=F32)


def dot_tn(lhs, rhs):
    return lax.dot_general(lhs, rhs, (((0,), (0,)), ((), ())), preferred_element_type=F32)


def dot_nt(lhs, rhs):
    return lax.dot_general(lhs, rhs, (((1,), (1,)), ((), ())), preferred_element_type=F32)


def dft_table(length):
    index = np.arange(length)
    turns = (index[:, None] * index[None, :]) % length
    angle = turns * (2.0 * np.pi / length)
    scale = 1.0 / np.sqrt(length)
    cos = np.cos(angle) * scale
    sin = np.sin(angle) * scale
    return np.block([[cos, sin], [-sin, cos]]).astype(np.float32).astype(BF16)


def depth_order(devices, x_local, slices):
    depth = devices * slices
    place = np.zeros((x_local, devices * x_local * slices * 2, 2 * depth), np.float32)
    for d in range(devices):
        for x in range(x_local):
            for z in range(slices):
                for p in range(2):
                    place[x, ((d * x_local + x) * slices + z) * 2 + p, p * depth + d * slices + z] = 1
    return place.reshape(-1, 2 * depth).astype(BF16)


def gather_order(slabs, coils, x_local, slices):
    rows = slabs * x_local
    place = np.zeros((slices * 2 * rows, slabs * coils * x_local * slices * 2), np.float32)
    for s in range(slabs):
        for c in range(coils):
            for x in range(x_local):
                for z in range(slices):
                    for p in range(2):
                        source = (((s * coils + c) * x_local + x) * slices + z) * 2 + p
                        place[(z * 2 + p) * rows + s * x_local + x, source] = 1
    return place.astype(BF16)


VMEM = pl.BlockSpec(memory_space=pltpu.VMEM)
HBM = pl.BlockSpec(memory_space=pltpu.HBM)


def call(kernel, out_shape, scratch=(), flops=0, nbytes=0, limit=VMEM_LIMIT, **kwargs):
    return pl.pallas_call(
        kernel,
        out_shape=out_shape,
        scratch_shapes=list(scratch),
        compiler_params=pltpu.CompilerParams(vmem_limit_bytes=limit),
        cost_estimate=pl.CostEstimate(flops=flops, bytes_accessed=nbytes, transcendentals=0),
        **kwargs,
    )


def split(values, count):
    if count & (count - 1) == 0:
        return values & (count - 1), lax.shift_right_logical(values, count.bit_length() - 1)
    return lax.rem(values, count), lax.div(values, count)


def pack_kernel(image_ref, blocks_ref):
    slices, parts, rows, cols = image_ref.shape
    copies = blocks_ref.shape[0] * blocks_ref.shape[1] // (slices * parts * rows)
    image = image_ref[...].astype(BF16)
    count = slices * parts * rows
    after = lax.broadcasted_iota(jnp.int32, (count, count), 0)
    before = lax.broadcasted_iota(jnp.int32, (count, count), 1)
    part, x = split(after, slices * parts)
    source_x, source_part = split(before, rows)
    order = jnp.where((part == source_part) & (x == source_x), 1.0, 0.0).astype(BF16)
    moved = dot(order, image.reshape(count, cols))
    slabs = blocks_ref.shape[0] // copies
    moved = moved.reshape(slabs, 1, blocks_ref.shape[1], cols)
    moved = jnp.broadcast_to(moved, (slabs, copies) + moved.shape[2:])
    blocks_ref[...] = moved.reshape(blocks_ref.shape).astype(BF16)


def halo_kernel(outward, image_ref, after_ref, out_ref):
    del after_ref
    slices = image_ref.shape[0]
    even = lax.axis_index("coil") % 2 == 0
    out_ref[...] = jnp.where(even != outward, image_ref[slices - 2 :], image_ref[:2]).astype(BF16)


def by_three(values):
    return lax.shift_right_logical(values * 11, 5)


def first_order():
    row = lax.broadcasted_iota(jnp.int32, (240, 256), 0)
    col = lax.broadcasted_iota(jnp.int32, (240, 256), 1)
    tap = lax.shift_right_logical(row, 3)
    a = jnp.where(tap >= 20, 2, jnp.where(tap >= 10, 1, 0))
    channel = tap - 10 * a
    group = lax.shift_right_logical(col, 3)
    offset = by_three(lax.shift_right_logical(group, 1))
    b = lax.shift_right_logical(group, 1) - 3 * offset
    same = (channel == 2 * offset + (group & 1)) & ((row & 7) == b) & ((col & 7) == a + 1)
    return jnp.where(same, 0.5, 0.0).astype(BF16)


def last_order():
    row = lax.broadcasted_iota(jnp.int32, (QUAD * 48, 72), 0)
    col = lax.broadcasted_iota(jnp.int32, (QUAD * 48, 72), 1)
    group = lax.shift_right_logical(row, 3)
    xo = by_three(lax.shift_right_logical(group, 1))
    b = lax.shift_right_logical(group, 1) - 3 * xo
    tap = lax.shift_right_logical(col, 3)
    a = by_three(tap)
    same = ((col & 7) == (group & 1)) & (tap - 3 * a == b) & (a == xo - (row & 7) + 3)
    return jnp.where(same, 1.0, 0.0).astype(BF16)


def fold_weights(sources, targets, rows):
    first_ref, b1_ref, second_ref, b2_ref, third_ref, b3_ref, last_ref = sources
    w1_ref, _, w2_ref, c2_ref, w3_ref, c3_ref, w4_ref = targets
    width = second_ref.shape[0]

    def padded(ref):
        rows[...] = jnp.zeros_like(rows)
        outer, inner, count, _ = ref.shape
        for i in range(outer):
            for j in range(inner):
                rows[i * inner + j, :count] = ref[i, j].astype(F32)
        return rows[: outer * inner].reshape(outer * inner * 8, width).astype(BF16)

    rest = jnp.transpose(jnp.broadcast_to(b1_ref[...] * 0.5, (width, width)))
    rest = jnp.concatenate([rest, rest], axis=1)
    lane = lax.broadcasted_iota(jnp.int32, rest.shape, 1)
    column = jnp.zeros_like(rest)
    for k in range(3):
        part = rest.astype(BF16).astype(F32)
        rest = rest - part
        column = jnp.where(lane == 240 + k, part, column)
    placed = dot_tn(padded(first_ref), first_order())
    for xo in range(QUAD):
        moved = pltpu.roll(placed, xo, 1) if xo else placed
        w1_ref[xo * width : (xo + 1) * width] = (moved + column).astype(BF16)
    placed = dot(last_order(), padded(last_ref)).astype(BF16)
    for xo in range(QUAD):
        w4_ref[:, xo * width : (xo + 1) * width] = placed[xo * 48 : (xo + 1) * 48]
    for source, target in ((second_ref, w2_ref), (third_ref, w3_ref)):
        turned = (jnp.transpose(source[...].astype(F32)) * 0.5).astype(BF16)
        zeros = jnp.zeros_like(turned)
        target[...] = jnp.concatenate(
            [jnp.concatenate([turned, zeros], axis=1), jnp.concatenate([zeros, turned], axis=1)], axis=0
        )
    for source, target in ((b2_ref, c2_ref), (b3_ref, c3_ref)):
        target[...] = jnp.transpose(jnp.broadcast_to(source[...] * 0.5, (width, width)))


def staggered(chains):
    waiting, running = list(chains), []
    while waiting or running:
        if waiting:
            running.append(waiting.pop(0))
        for one in running[::-1]:
            if next(one, one) is one:
                running.remove(one)


def half_silu(half):
    return (half + half * jnp.tanh(half)).astype(BF16)


def score_kernel(spots, sources, n_ordered, *refs):
    added = refs[sources : sources + n_ordered - 1]
    refs, out_ref, scratch = refs[:sources], refs[sources + n_ordered], refs[sources + n_ordered + 1 :]
    folded, rows, scratch = scratch[:7], scratch[7], scratch[8:]
    fold_weights(refs[3:], folded, rows)
    score_spots(spots, refs[:3], folded, added, out_ref, *scratch)


def score_spots(spots, planes, weights, added, out_ref, shifted, windows):
    image_ref, low_ref, high_ref = planes
    w1_ref, w2_ref, c2_ref, w3_ref, c3_ref, w4_ref = weights[:1] + weights[2:]
    slices, _, rows, cols = image_ref.shape
    quads = rows // QUAD
    width = c2_ref.shape[0]
    count = out_ref.shape[0]
    even = lax.axis_index("coil") % 2 == 0

    def plane_at(z, p, below_ref, above_ref):
        if 0 <= z < slices:
            return image_ref[z, p].astype(BF16).astype(F32)
        ref, at = (below_ref, z + 2) if z < 0 else (above_ref, z - slices)
        return ref[at, p].astype(F32)

    def plane(i, p):
        return jnp.where(
            even,
            plane_at(slices - count + i - 2, p, high_ref, low_ref),
            plane_at(i - 2, p, low_ref, high_ref),
        )

    def earlier(values):
        at = lax.broadcasted_iota(jnp.int32, values.shape, 1)
        return jnp.where(at == 0, 0.0, pltpu.roll(values, 1, 1))

    def later(values):
        at = lax.broadcasted_iota(jnp.int32, values.shape, 1)
        return jnp.where(at == cols - 1, 0.0, pltpu.roll(values, cols - 1, 1))

    shifted[...] = jnp.zeros_like(shifted)
    for i in range(count + 4):
        for p in range(2):
            values = plane(i, p)
            for b, moved in enumerate((earlier(values), values, later(values))):
                shifted[b, 4 : 4 + rows] = moved
                for q in range(quads):
                    start = QUAD * q + 2
                    windows[q, i, b, p * GROUP : (p + 1) * GROUP] = shifted[b, start : start + GROUP].astype(BF16)

    place = [jnp.where(even, count - 1 - i, i) for i in range(count)]
    ones = jnp.ones((16, cols), BF16)
    inputs = jnp.concatenate(
        [
            jnp.concatenate([windows[q, pl.ds(place[i], 5)].reshape(240, cols), ones], axis=0)
            for i, q in spots
        ],
        axis=1,
    )
    taps = {}
    fields = {}
    row = lax.broadcasted_iota(jnp.int32, (GROUP, cols), 0)

    def add_spot(n):
        i, q = spots[n]
        first, last = n * cols, (n + 1) * cols
        part = jnp.concatenate(
            [
                taps[m][:, max(first, m) - m : min(last, m + tile) - m]
                for m in range(first - first % tile, last, tile)
            ],
            axis=1,
        )
        total = part[16:32] + earlier(part[:16]) + later(part[32:])
        start = QUAD * q - 2
        for o in range(2):
            moved = pltpu.roll(total[o * GROUP : (o + 1) * GROUP], start % GROUP, 0)
            for t, keep in ((start // GROUP, row >= start % GROUP), (start // GROUP + 1, row < start % GROUP)):
                if 0 <= t < rows // GROUP:
                    field = fields.get((i, o, t))
                    piece = jnp.where(keep, moved, 0.0)
                    fields[i, o, t] = piece if field is None else field + piece
        if n + 1 == len(spots) or spots[n + 1][0] != i:
            for o in range(2):
                for t in range(rows // GROUP):
                    value = fields.pop((i, o, t), None)
                    value = jnp.zeros((GROUP, cols), F32) if value is None else value
                    at = (place[i], o, slice(t * GROUP, (t + 1) * GROUP))
                    if added:
                        noise_ref, one_ref = added
                        if i == 0:
                            value = value + one_ref[0, o, at[2]]
                        value = image_ref[at] + STEP_SIZE * value + noise_ref[at]
                    out_ref[at] = value

    def bias(ref, lanes):
        return jnp.concatenate([jnp.concatenate([ref[...]] * (lanes // 128), axis=1)] * 2, axis=0)

    def chain(start, stop, pair):
        half = slice(2 * width * pair, 2 * width * (pair + 1))
        lanes = stop - start
        total = dot(w1_ref[half], inputs[:, start:stop])
        yield
        hidden = half_silu(total)
        yield
        total = dot(w2_ref[...], hidden)
        yield
        hidden = half_silu(total + bias(c2_ref, lanes))
        yield
        total = dot(w3_ref[...], hidden)
        yield
        hidden = half_silu(total + bias(c3_ref, lanes))
        yield
        part = dot(w4_ref[:, half], hidden)
        if pair == 0:
            taps[start] = part
            return
        taps[start] = taps[start] + part
        while done[0] < len(spots) and stop >= (done[0] + 1) * cols:
            add_spot(done[0])
            done[0] += 1

    done = [0]
    length = len(spots) * cols
    tile = 256
    staggered([chain(n, min(n + tile, length), pair) for n in range(0, length, tile) for pair in range(QUAD // 2)])


def adjoint_kernel(
    planes_ref, sens_ref, measured_hbm, mask_ref, half_ref, z_ref, out_ref, y_ref, measured_ref, sems
):
    blocks, block_rows, cols = planes_ref.shape
    coils, _, x_local, _, depth = sens_ref.shape
    per = max(1, 512 // depth)
    groups = [range(c, min(c + per, coils)) for c in range(0, coils, per)]
    arrivals = {}
    for i, group in enumerate(groups):
        part = pl.ds(group[0], len(group))
        arrivals[group] = pltpu.make_async_copy(measured_hbm.at[part], measured_ref.at[part], sems.at[i])
        arrivals[group].start()
    y_ref[:cols] = half_ref[...]
    y_ref[cols:, :cols] = -half_ref[:, cols:]
    y_ref[cols:, cols:] = half_ref[:, :cols]
    received = planes_ref[...].astype(F32).reshape(blocks * block_rows, cols).astype(BF16)
    z_table = z_ref[: 2 * depth]
    result = None
    for x in range(x_local):
        place = z_ref[2 * depth + x * blocks * block_rows : 2 * depth + (x + 1) * blocks * block_rows]
        planes = dot_tn(received, place)
        image_real = planes[:, :depth]
        image_imag = planes[:, depth:]
        totals = {}

        def along_z(half, count):
            for i in range(count):
                at = slice(i * depth, (i + 1) * depth)
                yield dot(jnp.concatenate([half[:cols, at], half[cols:, at]], axis=1), z_table)

        def stack(top, bottom):
            return jnp.concatenate([jnp.concatenate(top, axis=1), jnp.concatenate(bottom, axis=1)], axis=0)

        bands = [slice(r, min(r + BAND, cols)) for r in range(0, cols, BAND)]

        def chain(group):
            reals = {c: [] for c in group}
            imags = {c: [] for c in group}

            def joined(parts):
                return [jnp.concatenate(parts[c], axis=0) for c in group]

            for band in bands:
                for c in group:
                    sens_real = sens_ref[c, 0, x, band].astype(F32)
                    sens_imag = sens_ref[c, 1, x, band].astype(F32)
                    reals[c].append((sens_real * image_real[band] - sens_imag * image_imag[band]).astype(BF16))
                    imags[c].append((sens_real * image_imag[band] + sens_imag * image_real[band]).astype(BF16))
            stacked = stack(joined(reals), joined(imags))
            yield
            half = dot(y_ref[...], stacked).astype(BF16)
            yield
            specs = list(along_z(half, len(group)))
            yield
            if x == 0:
                arrivals[group].wait()
            reals = {c: [] for c in group}
            imags = {c: [] for c in group}
            for band in bands:
                sampled = mask_ref[band].astype(F32)
                for spec, c in zip(specs, group):
                    measured_real = measured_ref[c, 0, x, band].astype(F32)
                    measured_imag = measured_ref[c, 1, x, band].astype(F32)
                    reals[c].append((sampled * (spec[band, :depth] - measured_real)).astype(BF16))
                    imags[c].append((sampled * (spec[band, depth:] - measured_imag)).astype(BF16))
            stacked = stack(joined(imags), joined(reals))
            yield
            half = dot(y_ref[...], stacked).astype(BF16)
            yield
            backs = list(along_z(half, len(group)))
            yield
            for band in bands:
                real = imag = None
                for back, c in zip(backs, group):
                    back_imag = back[band, :depth]
                    back_real = back[band, depth:]
                    sens_real = sens_ref[c, 0, x, band].astype(F32)
                    sens_imag = sens_ref[c, 1, x, band].astype(F32)
                    one = sens_real * back_real + sens_imag * back_imag
                    two = sens_real * back_imag - sens_imag * back_real
                    real, imag = (one, two) if real is None else (real + one, imag + two)
                totals.setdefault(band.start, []).append((real, imag))

        staggered([chain(group) for group in groups])
        total = jnp.concatenate(
            [
                jnp.concatenate([sum(t[part] for t in totals[band.start]) for part in range(2)], axis=1)
                for band in bands
            ],
            axis=0,
        ).astype(BF16)
        placed = dot_nt(place, total)
        result = placed if result is None else result + placed
    out_ref[...] = result.reshape(out_ref.shape).astype(BF16)


def final_kernel(moved_ref, back_ref, order_ref, out_ref):
    blocks, block_rows, cols = back_ref.shape
    received = back_ref[...].astype(F32).reshape(blocks * block_rows, cols).astype(BF16)
    gradient = dot(order_ref[...], received).reshape(moved_ref.shape)
    out_ref[...] = moved_ref[...] - STEP_SIZE * gradient


def on_device(
    image, noise, sens, measured, mask, w_first, b_first, w_second, b_second, w_third, b_third, w_last
):
    slabs = lax.axis_size("slab")
    groups = lax.axis_size("coil")
    devices = slabs * groups
    slices, _, rows, cols = image.shape
    x_local = rows // slabs
    width = w_second.shape[0]
    depth = sens.shape[4]
    both = ("slab", "coil")
    block = jax.ShapeDtypeStruct((devices, x_local * slices * 2, cols), BF16)

    blocks = call(pack_kernel, block, flops=BUSY, nbytes=10**6, in_specs=[VMEM])(image)
    pairs = [(i, i ^ 1) for i in range(devices)]
    across = [(i, ((i + 1) ^ 1) - 1) for i in range(1, devices - 1)]

    def halo(outward, after):
        kernel = functools.partial(halo_kernel, outward)
        shape = jax.ShapeDtypeStruct((2, 2, rows, cols), BF16)
        slab = call(
            kernel, shape, flops=BUSY, nbytes=10**6, in_specs=[VMEM, pl.BlockSpec(memory_space=pl.ANY)]
        )(image, after)
        return lax.ppermute(slab, both, across if outward else pairs)

    low = halo(False, blocks)
    planes = lax.all_to_all(blocks, both, split_axis=0, concat_axis=0, tiled=True)

    weights = (
        jnp.transpose(w_first, (0, 2, 1, 3)), b_first[None],
        w_second, b_second[None], w_third, b_third[None], w_last,
    )

    def score(spots, count, flops, planes, *ordered):
        sources = planes + weights
        return call(
            lambda *refs: score_kernel(spots, len(sources), len(ordered), *refs),
            jax.ShapeDtypeStruct((count, 2, rows, cols), F32),
            [
                pltpu.VMEM((QUAD * width, 256), BF16),
                pltpu.VMEM((8, width), F32),
                pltpu.VMEM((2 * width, 2 * width), BF16),
                pltpu.VMEM((width, width), F32),
                pltpu.VMEM((2 * width, 2 * width), BF16),
                pltpu.VMEM((width, width), F32),
                pltpu.VMEM((48, QUAD * width), BF16),
                pltpu.VMEM((30, 8, width), F32),
                pltpu.VMEM((3, rows + 8, cols), F32),
                pltpu.VMEM((rows // QUAD, count + 4, 3, 2 * GROUP, cols), BF16),
            ],
            flops=flops,
            nbytes=2 * 10**6,
            in_specs=[VMEM] * (len(sources) + max(0, len(ordered) - 1))
            + [pl.BlockSpec(memory_space=pl.ANY)] * min(1, len(ordered)),
        )(*sources, *ordered)

    spots = [(i, q) for i in range(slices) for q in range(rows // QUAD)]
    early = rows // QUAD * EARLY // 4
    apart = slices >= 3
    high = None if apart else halo(True, blocks)
    score_one = score(spots[:early], 1, SHORT, (image, low, low if apart else high))
    if apart:
        high = halo(True, score_one)
    z_tables = np.concatenate([dft_table(depth).T, depth_order(devices, x_local, slices)], axis=0)
    partial = call(
        adjoint_kernel, block, [pltpu.VMEM((2 * cols, 2 * cols), BF16), pltpu.VMEM(measured.shape, BF16),
         pltpu.SemaphoreType.DMA((sens.shape[0],))],
        flops=BUSY, nbytes=5 * 10**6, limit=WIDE_LIMIT, in_specs=[VMEM] * 2 + [HBM] + [VMEM] * 3
    )(planes, sens, measured, mask, jnp.asarray(dft_table(cols)[:cols]), jnp.asarray(z_tables))
    moved = score(spots[early:], slices, BUSY, (image, low, high), noise, score_one, partial)
    back = lax.all_to_all(partial, both, split_axis=0, concat_axis=0, tiled=True)
    return call(final_kernel, jax.ShapeDtypeStruct(image.shape, F32), nbytes=10**6)(
        moved, back,
        jnp.asarray(gather_order(slabs, groups, x_local, slices)),
    )


def solution(mesh):
    whole = P(("slab", "coil"), None, None, None)
    by_coil = P("coil", None, "slab", None, None)
    return jax.shard_map(
        on_device,
        mesh=mesh,
        in_specs=(whole, whole, by_coil, by_coil) + (P(),) * 8,
        out_specs=whole,
        check_vma=False,
    )
```

```python
import functools

import jax
import jax.numpy as jnp
import numpy as np
from jax import lax
from jax.experimental import pallas as pl
from jax.experimental.pallas import tpu as pltpu
from jax.sharding import PartitionSpec as P

STEP_SIZE = 0.5
F32 = jnp.float32
BF16 = jnp.bfloat16
QUAD = 4
GROUP = 8
VMEM_LIMIT = 24 * 2**20
WIDE_LIMIT = 100 * 2**19
BUSY = 4 * 10**10
SHORT = BUSY
BAND = 64
EARLY = 3


def dot(lhs, rhs):
    return jnp.dot(lhs, rhs, preferred_element_type=F32)


def dot_tn(lhs, rhs):
    return lax.dot_general(lhs, rhs, (((0,), (0,)), ((), ())), preferred_element_type=F32)


def dot_nt(lhs, rhs):
    return lax.dot_general(lhs, rhs, (((1,), (1,)), ((), ())), preferred_element_type=F32)


def dft_table(length):
    index = np.arange(length)
    turns = (index[:, None] * index[None, :]) % length
    angle = turns * (2.0 * np.pi / length)
    scale = 1.0 / np.sqrt(length)
    cos = np.cos(angle) * scale
    sin = np.sin(angle) * scale
    return np.block([[cos, sin], [-sin, cos]]).astype(np.float32).astype(BF16)


def depth_order(devices, x_local, slices):
    depth = devices * slices
    place = np.zeros((x_local, devices * x_local * slices * 2, 2 * depth), np.float32)
    for d in range(devices):
        for x in range(x_local):
            for z in range(slices):
                for p in range(2):
                    place[x, ((d * x_local + x) * slices + z) * 2 + p, p * depth + d * slices + z] = 1
    return place.reshape(-1, 2 * depth).astype(BF16)


def gather_order(slabs, coils, x_local, slices):
    rows = slabs * x_local
    place = np.zeros((slices * 2 * rows, slabs * coils * x_local * slices * 2), np.float32)
    for s in range(slabs):
        for c in range(coils):
            for x in range(x_local):
                for z in range(slices):
                    for p in range(2):
                        source = (((s * coils + c) * x_local + x) * slices + z) * 2 + p
                        place[(z * 2 + p) * rows + s * x_local + x, source] = 1
    return place.astype(BF16)


VMEM = pl.BlockSpec(memory_space=pltpu.VMEM)
HBM = pl.BlockSpec(memory_space=pltpu.HBM)


def call(kernel, out_shape, scratch=(), flops=0, nbytes=0, limit=VMEM_LIMIT, **kwargs):
    return pl.pallas_call(
        kernel,
        out_shape=out_shape,
        scratch_shapes=list(scratch),
        compiler_params=pltpu.CompilerParams(vmem_limit_bytes=limit),
        cost_estimate=pl.CostEstimate(flops=flops, bytes_accessed=nbytes, transcendentals=0),
        **kwargs,
    )


def split(values, count):
    if count & (count - 1) == 0:
        return values & (count - 1), lax.shift_right_logical(values, count.bit_length() - 1)
    return lax.rem(values, count), lax.div(values, count)


def pack_kernel(image_ref, blocks_ref):
    slices, parts, rows, cols = image_ref.shape
    copies = blocks_ref.shape[0] * blocks_ref.shape[1] // (slices * parts * rows)
    image = image_ref[...].astype(BF16)
    count = slices * parts * rows
    after = lax.broadcasted_iota(jnp.int32, (count, count), 0)
    before = lax.broadcasted_iota(jnp.int32, (count, count), 1)
    part, x = split(after, slices * parts)
    source_x, source_part = split(before, rows)
    order = jnp.where((part == source_part) & (x == source_x), 1.0, 0.0).astype(BF16)
    moved = dot(order, image.reshape(count, cols))
    slabs = blocks_ref.shape[0] // copies
    moved = moved.reshape(slabs, 1, blocks_ref.shape[1], cols)
    moved = jnp.broadcast_to(moved, (slabs, copies) + moved.shape[2:])
    blocks_ref[...] = moved.reshape(blocks_ref.shape).astype(BF16)


def halo_kernel(outward, image_ref, after_ref, out_ref):
    del after_ref
    slices = image_ref.shape[0]
    even = lax.axis_index("coil") % 2 == 0
    out_ref[...] = jnp.where(even != outward, image_ref[slices - 2 :], image_ref[:2]).astype(BF16)


def by_three(values):
    return lax.shift_right_logical(values * 11, 5)


def first_order():
    row = lax.broadcasted_iota(jnp.int32, (240, 256), 0)
    col = lax.broadcasted_iota(jnp.int32, (240, 256), 1)
    tap = lax.shift_right_logical(row, 3)
    a = jnp.where(tap >= 20, 2, jnp.where(tap >= 10, 1, 0))
    channel = tap - 10 * a
    group = lax.shift_right_logical(col, 3)
    offset = by_three(lax.shift_right_logical(group, 1))
    b = lax.shift_right_logical(group, 1) - 3 * offset
    same = (channel == 2 * offset + (group & 1)) & ((row & 7) == b) & ((col & 7) == a + 1)
    return jnp.where(same, 0.5, 0.0).astype(BF16)


def last_order():
    row = lax.broadcasted_iota(jnp.int32, (QUAD * 48, 72), 0)
    col = lax.broadcasted_iota(jnp.int32, (QUAD * 48, 72), 1)
    group = lax.shift_right_logical(row, 3)
    xo = by_three(lax.shift_right_logical(group, 1))
    b = lax.shift_right_logical(group, 1) - 3 * xo
    tap = lax.shift_right_logical(col, 3)
    a = by_three(tap)
    same = ((col & 7) == (group & 1)) & (tap - 3 * a == b) & (a == xo - (row & 7) + 3)
    return jnp.where(same, 1.0, 0.0).astype(BF16)


def fold_weights(sources, targets, rows):
    first_ref, b1_ref, second_ref, b2_ref, third_ref, b3_ref, last_ref = sources
    w1_ref, _, w2_ref, c2_ref, w3_ref, c3_ref, w4_ref = targets
    width = second_ref.shape[0]

    def padded(ref):
        rows[...] = jnp.zeros_like(rows)
        outer, inner, count, _ = ref.shape
        for i in range(outer):
            for j in range(inner):
                rows[i * inner + j, :count] = ref[i, j].astype(F32)
        return rows[: outer * inner].reshape(outer * inner * 8, width).astype(BF16)

    rest = jnp.transpose(jnp.broadcast_to(b1_ref[...] * 0.5, (width, width)))
    rest = jnp.concatenate([rest, rest], axis=1)
    lane = lax.broadcasted_iota(jnp.int32, rest.shape, 1)
    column = jnp.zeros_like(rest)
    for k in range(3):
        part = rest.astype(BF16).astype(F32)
        rest = rest - part
        column = jnp.where(lane == 240 + k, part, column)
    placed = dot_tn(padded(first_ref), first_order())
    for xo in range(QUAD):
        moved = pltpu.roll(placed, xo, 1) if xo else placed
        w1_ref[xo * width : (xo + 1) * width] = (moved + column).astype(BF16)
    placed = dot(last_order(), padded(last_ref)).astype(BF16)
    for xo in range(QUAD):
        w4_ref[:, xo * width : (xo + 1) * width] = placed[xo * 48 : (xo + 1) * 48]
    for source, target in ((second_ref, w2_ref), (third_ref, w3_ref)):
        turned = (jnp.transpose(source[...].astype(F32)) * 0.5).astype(BF16)
        zeros = jnp.zeros_like(turned)
        target[...] = jnp.concatenate(
            [jnp.concatenate([turned, zeros], axis=1), jnp.concatenate([zeros, turned], axis=1)], axis=0
        )
    for source, target in ((b2_ref, c2_ref), (b3_ref, c3_ref)):
        target[...] = jnp.transpose(jnp.broadcast_to(source[...] * 0.5, (width, width)))


def staggered(chains):
    waiting, running = list(chains), []
    while waiting or running:
        if waiting:
            running.append(waiting.pop(0))
        for one in running[::-1]:
            if next(one, one) is one:
                running.remove(one)


def half_silu(half):
    return (half + half * jnp.tanh(half)).astype(BF16)


def score_kernel(spots, sources, n_ordered, *refs):
    added = refs[sources : sources + n_ordered - 1]
    refs, out_ref, scratch = refs[:sources], refs[sources + n_ordered], refs[sources + n_ordered + 1 :]
    folded, rows, scratch = scratch[:7], scratch[7], scratch[8:]
    fold_weights(refs[3:], folded, rows)
    score_spots(spots, refs[:3], folded, added, out_ref, *scratch)


def score_spots(spots, planes, weights, added, out_ref, shifted, windows):
    image_ref, low_ref, high_ref = planes
    w1_ref, w2_ref, c2_ref, w3_ref, c3_ref, w4_ref = weights[:1] + weights[2:]
    slices, _, rows, cols = image_ref.shape
    quads = rows // QUAD
    width = c2_ref.shape[0]
    count = out_ref.shape[0]
    even = lax.axis_index("coil") % 2 == 0

    def plane_at(z, p, below_ref, above_ref):
        if 0 <= z < slices:
            return image_ref[z, p].astype(BF16).astype(F32)
        ref, at = (below_ref, z + 2) if z < 0 else (above_ref, z - slices)
        return ref[at, p].astype(F32)

    def plane(i, p):
        return jnp.where(
            even,
            plane_at(slices - count + i - 2, p, high_ref, low_ref),
            plane_at(i - 2, p, low_ref, high_ref),
        )

    def earlier(values):
        at = lax.broadcasted_iota(jnp.int32, values.shape, 1)
        return jnp.where(at == 0, 0.0, pltpu.roll(values, 1, 1))

    def later(values):
        at = lax.broadcasted_iota(jnp.int32, values.shape, 1)
        return jnp.where(at == cols - 1, 0.0, pltpu.roll(values, cols - 1, 1))

    shifted[...] = jnp.zeros_like(shifted)
    for i in range(count + 4):
        for p in range(2):
            values = plane(i, p)
            for b, moved in enumerate((earlier(values), values, later(values))):
                shifted[b, 4 : 4 + rows] = moved
                for q in range(quads):
                    start = QUAD * q + 2
                    windows[q, i, b, p * GROUP : (p + 1) * GROUP] = shifted[b, start : start + GROUP].astype(BF16)

    place = [jnp.where(even, count - 1 - i, i) for i in range(count)]
    ones = jnp.ones((16, cols), BF16)
    inputs = jnp.concatenate(
        [
            jnp.concatenate([windows[q, pl.ds(place[i], 5)].reshape(240, cols), ones], axis=0)
            for i, q in spots
        ],
        axis=1,
    )
    taps = {}
    fields = {}
    row = lax.broadcasted_iota(jnp.int32, (GROUP, cols), 0)

    def add_spot(n):
        i, q = spots[n]
        first, last = n * cols, (n + 1) * cols
        part = jnp.concatenate(
            [
                taps[m][:, max(first, m) - m : min(last, m + tile) - m]
                for m in range(first - first % tile, last, tile)
            ],
            axis=1,
        )
        total = part[16:32] + earlier(part[:16]) + later(part[32:])
        start = QUAD * q - 2
        for o in range(2):
            moved = pltpu.roll(total[o * GROUP : (o + 1) * GROUP], start % GROUP, 0)
            for t, keep in ((start // GROUP, row >= start % GROUP), (start // GROUP + 1, row < start % GROUP)):
                if 0 <= t < rows // GROUP:
                    field = fields.get((i, o, t))
                    piece = jnp.where(keep, moved, 0.0)
                    fields[i, o, t] = piece if field is None else field + piece
        if n + 1 == len(spots) or spots[n + 1][0] != i:
            for o in range(2):
                for t in range(rows // GROUP):
                    value = fields.pop((i, o, t), None)
                    value = jnp.zeros((GROUP, cols), F32) if value is None else value
                    at = (place[i], o, slice(t * GROUP, (t + 1) * GROUP))
                    if added:
                        noise_ref, one_ref = added
                        if i == 0:
                            value = value + one_ref[0, o, at[2]]
                        value = image_ref[at] + STEP_SIZE * value + noise_ref[at]
                    out_ref[at] = value

    def bias(ref, lanes):
        return jnp.concatenate([jnp.concatenate([ref[...]] * (lanes // 128), axis=1)] * 2, axis=0)

    def chain(start, stop, pair):
        half = slice(2 * width * pair, 2 * width * (pair + 1))
        lanes = stop - start
        total = dot(w1_ref[half], inputs[:, start:stop])
        yield
        hidden = half_silu(total)
        yield
        total = dot(w2_ref[...], hidden)
        yield
        hidden = half_silu(total + bias(c2_ref, lanes))
        yield
        total = dot(w3_ref[...], hidden)
        yield
        hidden = half_silu(total + bias(c3_ref, lanes))
        yield
        part = dot(w4_ref[:, half], hidden)
        if pair == 0:
            taps[start] = part
            return
        taps[start] = taps[start] + part
        while done[0] < len(spots) and stop >= (done[0] + 1) * cols:
            add_spot(done[0])
            done[0] += 1

    done = [0]
    length = len(spots) * cols
    tile = 256
    staggered([chain(n, min(n + tile, length), pair) for n in range(0, length, tile) for pair in range(QUAD // 2)])


def adjoint_kernel(
    planes_ref, sens_ref, measured_hbm, mask_ref, half_ref, z_ref, out_ref, y_ref, measured_ref, sems
):
    blocks, block_rows, cols = planes_ref.shape
    coils, _, x_local, _, depth = sens_ref.shape
    per = max(1, 512 // depth)
    groups = [range(c, min(c + per, coils)) for c in range(0, coils, per)]
    arrivals = {}
    for i, group in enumerate(groups):
        part = pl.ds(group[0], len(group))
        arrivals[group] = pltpu.make_async_copy(measured_hbm.at[part], measured_ref.at[part], sems.at[i])
        arrivals[group].start()
    y_ref[:cols] = half_ref[...]
    y_ref[cols:, :cols] = -half_ref[:, cols:]
    y_ref[cols:, cols:] = half_ref[:, :cols]
    received = planes_ref[...].astype(F32).reshape(blocks * block_rows, cols).astype(BF16)
    z_table = z_ref[: 2 * depth]
    result = None
    for x in range(x_local):
        place = z_ref[2 * depth + x * blocks * block_rows : 2 * depth + (x + 1) * blocks * block_rows]
        planes = dot_tn(received, place)
        image_real = planes[:, :depth]
        image_imag = planes[:, depth:]
        totals = {}

        def along_z(half, count):
            for i in range(count):
                at = slice(i * depth, (i + 1) * depth)
                yield dot(jnp.concatenate([half[:cols, at], half[cols:, at]], axis=1), z_table)

        def stack(top, bottom):
            return jnp.concatenate([jnp.concatenate(top, axis=1), jnp.concatenate(bottom, axis=1)], axis=0)

        bands = [slice(r, min(r + BAND, cols)) for r in range(0, cols, BAND)]

        def chain(group):
            reals = {c: [] for c in group}
            imags = {c: [] for c in group}

            def joined(parts):
                return [jnp.concatenate(parts[c], axis=0) for c in group]

            for band in bands:
                for c in group:
                    sens_real = sens_ref[c, 0, x, band].astype(F32)
                    sens_imag = sens_ref[c, 1, x, band].astype(F32)
                    reals[c].append((sens_real * image_real[band] - sens_imag * image_imag[band]).astype(BF16))
                    imags[c].append((sens_real * image_imag[band] + sens_imag * image_real[band]).astype(BF16))
            stacked = stack(joined(reals), joined(imags))
            yield
            half = dot(y_ref[...], stacked).astype(BF16)
            yield
            specs = list(along_z(half, len(group)))
            yield
            if x == 0:
                arrivals[group].wait()
            reals = {c: [] for c in group}
            imags = {c: [] for c in group}
            for band in bands:
                sampled = mask_ref[band].astype(F32)
                for spec, c in zip(specs, group):
                    measured_real = measured_ref[c, 0, x, band].astype(F32)
                    measured_imag = measured_ref[c, 1, x, band].astype(F32)
                    reals[c].append((sampled * (spec[band, :depth] - measured_real)).astype(BF16))
                    imags[c].append((sampled * (spec[band, depth:] - measured_imag)).astype(BF16))
            stacked = stack(joined(imags), joined(reals))
            yield
            half = dot(y_ref[...], stacked).astype(BF16)
            yield
            backs = list(along_z(half, len(group)))
            yield
            for band in bands:
                real = imag = None
                for back, c in zip(backs, group):
                    back_imag = back[band, :depth]
                    back_real = back[band, depth:]
                    sens_real = sens_ref[c, 0, x, band].astype(F32)
                    sens_imag = sens_ref[c, 1, x, band].astype(F32)
                    one = sens_real * back_real + sens_imag * back_imag
                    two = sens_real * back_imag - sens_imag * back_real
                    real, imag = (one, two) if real is None else (real + one, imag + two)
                totals.setdefault(band.start, []).append((real, imag))

        staggered([chain(group) for group in groups])
        total = jnp.concatenate(
            [
                jnp.concatenate([sum(t[part] for t in totals[band.start]) for part in range(2)], axis=1)
                for band in bands
            ],
            axis=0,
        ).astype(BF16)
        placed = dot_nt(place, total)
        result = placed if result is None else result + placed
    out_ref[...] = result.reshape(out_ref.shape).astype(BF16)


def final_kernel(moved_ref, back_ref, order_ref, out_ref):
    blocks, block_rows, cols = back_ref.shape
    received = back_ref[...].astype(F32).reshape(blocks * block_rows, cols).astype(BF16)
    gradient = dot(order_ref[...], received).reshape(moved_ref.shape)
    out_ref[...] = moved_ref[...] - STEP_SIZE * gradient


def on_device(
    image, noise, sens, measured, mask, w_first, b_first, w_second, b_second, w_third, b_third, w_last
):
    slabs = lax.axis_size("slab")
    groups = lax.axis_size("coil")
    devices = slabs * groups
    slices, _, rows, cols = image.shape
    x_local = rows // slabs
    width = w_second.shape[0]
    depth = sens.shape[4]
    both = ("slab", "coil")
    block = jax.ShapeDtypeStruct((devices, x_local * slices * 2, cols), BF16)

    blocks = call(pack_kernel, block, flops=BUSY, nbytes=10**6, in_specs=[VMEM])(image)
    pairs = [(i, i ^ 1) for i in range(devices)]
    across = [(i, ((i + 1) ^ 1) - 1) for i in range(1, devices - 1)]

    def halo(outward, after):
        kernel = functools.partial(halo_kernel, outward)
        shape = jax.ShapeDtypeStruct((2, 2, rows, cols), BF16)
        slab = call(
            kernel, shape, flops=BUSY, nbytes=10**6, in_specs=[VMEM, pl.BlockSpec(memory_space=pl.ANY)]
        )(image, after)
        return lax.ppermute(slab, both, across if outward else pairs)

    low = halo(False, blocks)
    planes = lax.all_to_all(blocks, both, split_axis=0, concat_axis=0, tiled=True)

    weights = (
        jnp.transpose(w_first, (0, 2, 1, 3)), b_first[None],
        w_second, b_second[None], w_third, b_third[None], w_last,
    )

    def score(spots, count, flops, planes, *ordered):
        sources = planes + weights
        return call(
            lambda *refs: score_kernel(spots, len(sources), len(ordered), *refs),
            jax.ShapeDtypeStruct((count, 2, rows, cols), F32),
            [
                pltpu.VMEM((QUAD * width, 256), BF16),
                pltpu.VMEM((8, width), F32),
                pltpu.VMEM((2 * width, 2 * width), BF16),
                pltpu.VMEM((width, width), F32),
                pltpu.VMEM((2 * width, 2 * width), BF16),
                pltpu.VMEM((width, width), F32),
                pltpu.VMEM((48, QUAD * width), BF16),
                pltpu.VMEM((30, 8, width), F32),
                pltpu.VMEM((3, rows + 8, cols), F32),
                pltpu.VMEM((rows // QUAD, count + 4, 3, 2 * GROUP, cols), BF16),
            ],
            flops=flops,
            nbytes=2 * 10**6,
            in_specs=[VMEM] * (len(sources) + max(0, len(ordered) - 1))
            + [pl.BlockSpec(memory_space=pl.ANY)] * min(1, len(ordered)),
        )(*sources, *ordered)

    spots = [(i, q) for i in range(slices) for q in range(rows // QUAD)]
    early = rows // QUAD * EARLY // 4
    apart = slices >= 3
    high = None if apart else halo(True, blocks)
    score_one = score(spots[:early], 1, SHORT, (image, low, low if apart else high))
    if apart:
        high = halo(True, score_one)
    z_tables = np.concatenate([dft_table(depth).T, depth_order(devices, x_local, slices)], axis=0)
    partial = call(
        adjoint_kernel, block, [pltpu.VMEM((2 * cols, 2 * cols), BF16), pltpu.VMEM(measured.shape, BF16),
         pltpu.SemaphoreType.DMA((sens.shape[0],))],
        flops=BUSY, nbytes=5 * 10**6, limit=WIDE_LIMIT, in_specs=[VMEM] * 2 + [HBM] + [VMEM] * 3
    )(planes, sens, measured, mask, jnp.asarray(dft_table(cols)[:cols]), jnp.asarray(z_tables))
    moved = score(spots[early:], slices, BUSY, (image, low, high), noise, score_one, partial)
    back = lax.all_to_all(partial, both, split_axis=0, concat_axis=0, tiled=True)
    return call(final_kernel, jax.ShapeDtypeStruct(image.shape, F32), nbytes=10**6)(
        moved, back,
        jnp.asarray(gather_order(slabs, groups, x_local, slices)),
    )


def solution(mesh):
    whole = P(("slab", "coil"), None, None, None)
    by_coil = P("coil", None, "slab", None, None)
    return jax.shard_map(
        on_device,
        mesh=mesh,
        in_specs=(whole, whole, by_coil, by_coil) + (P(),) * 8,
        out_specs=whole,
        check_vma=False,
    )
```
